512 devices in a mesh: dp: 64 (over x, z), mp: 8 (over y, core).
Axes of the slice: x: 4, y: 4, z: 16, core: 2. Of those that a mesh axis runs over, the one named last changes fastest.
Arguments:
- query: bfloat16 [1024, 32, 8192], P('dp', None, 'mp'), may hold values from -30 to 30
- comp_key: bfloat16 [1024, 32, 1024], P('dp', None, 'mp'), may hold values from -6 to 6
- comp_value: bfloat16 [1024, 32, 1024], P('dp', None, 'mp'), may hold values from -6 to 6
- prefix_key: bfloat16 [64, 1024, 1024], P('dp', 'mp'), may hold values from -6 to 6
- prefix_value: bfloat16 [64, 1024, 1024], P('dp', 'mp'), may hold values from -6 to 6
- grad_out: bfloat16 [1024, 32, 8192], P('dp', None, 'mp'), may hold values from -6 to 6
- owner: int32 [64], replicated, may hold values from 0 to 63, as said below
- group: int32 [1024], P('dp'), may hold values from 0 to 63, as said below
- lengths: int32 [1024], P('dp'), may hold values from 1 to 32, as said below
Outputs:
- grad_query: bfloat16 [1024, 32, 8192], P('dp', None, 'mp')
- grad_comp_key: bfloat16 [1024, 32, 1024], P('dp', None, 'mp')
- grad_comp_value: bfloat16 [1024, 32, 1024], P('dp', None, 'mp')
- grad_prefix_key: bfloat16 [64, 1024, 1024], P('dp', 'mp')
- grad_prefix_value: bfloat16 [64, 1024, 1024], P('dp', 'mp')
The draws below stay inside these ranges and needn't reach their ends.
Inputs may be any that keep to these rules, and one draw needn't show every extreme that they name: `owner`: a permutation: every dp index owns exactly one prompt. `group`: every prompt has exactly 16 completions; the owner of the prompt of a completion held by dp index d is one of d - 2, d - 1, d, d + 1, d + 2 taken cyclically, and every dp index holds at least one completion of a prompt owned by each of d - 2, d - 1, d + 1, d + 2. `lengths`: every dp index holds at least one completion of 32 tokens.
All inputs are finite; a program needn't handle non-finite values.
Results may differ from the reference program's by a relative error of at most 0.012.
The reference program's roundings to bfloat16 on the way count: a program that leaves them out, or rounds other values in their place, can miss the bound.
Values may be sent and summed in bfloat16 or wider, within the bound.
No kernel may reach another device: no remote copies, remote signals or barrier semaphores. Data moves between devices by JAX's collectives and lax.ppermute only.
A program may use at most 64 MiB of HBM per device.

```python
import jax
import jax.numpy as jnp
from jax import lax

QH = 64
KVH = 8
HD = 128
LP = 1024
LC = 32
GROUP = 16
PROMPTS = 64
COMP = 1024


def placement_table(key):
    owner = jax.random.permutation(jax.random.fold_in(key, 101), PROMPTS).astype(jnp.int32)
    inverse = jnp.argsort(owner).astype(jnp.int32)
    devices = jnp.arange(PROMPTS, dtype=jnp.int32)
    fixed = jnp.stack([(devices - 2) % PROMPTS, (devices - 1) % PROMPTS, (devices + 1) % PROMPTS, (devices + 2) % PROMPTS], axis=1).astype(jnp.int32)
    spare = GROUP - 4
    source = jnp.broadcast_to(devices[:, None], (PROMPTS, spare))
    position = jnp.arange(spare, dtype=jnp.int32)[None, None, :]
    first = jax.random.randint(jax.random.fold_in(key, 102), (PROMPTS // 2, 1, 1), 1, spare + 1)
    paired = source.reshape(PROMPTS // 2, 2, spare)
    source = jnp.where(position < first, paired[:, ::-1, :], paired).reshape(PROMPTS, spare)
    second = jax.random.randint(jax.random.fold_in(key, 103), (PROMPTS // 2, 1, 1), 1, spare + 1)
    paired = jnp.roll(source, -1, axis=0).reshape(PROMPTS // 2, 2, spare)
    rolled = jnp.where(position < second, paired[:, ::-1, :], paired).reshape(PROMPTS, spare)
    source = jnp.roll(rolled, 1, axis=0)
    source = jnp.concatenate([fixed, source], axis=1)
    source = jax.random.permutation(jax.random.fold_in(key, 104), source, axis=1, independent=True)
    group = inverse[source].reshape(-1).astype(jnp.int32)
    return (owner, group)


def draw_owner(key, part):
    owner, group = placement_table(key)
    return owner


def draw_group(key, part):
    owner, group = placement_table(key)
    return group


def draw_lengths(key, part):
    key = jax.random.fold_in(key, 3)
    base = jax.random.randint(jax.random.fold_in(key, 1), (PROMPTS, GROUP), 1, LC + 1)
    picked = jax.random.randint(jax.random.fold_in(key, 2), (PROMPTS, 1), 0, GROUP)
    full = jnp.arange(GROUP)[None, :] == picked
    return jnp.where(full, LC, base).reshape(-1).astype(jnp.int32)


def draw_query(key, part):
    key = jax.random.fold_in(key, 5)
    values = jnp.clip(jax.random.normal(key, (COMP, LC, QH * HD), jnp.float32), -6.0, 6.0)
    return values.astype(jnp.bfloat16)


def draw_prefix_key(key, part):
    key = jax.random.fold_in(key, 6)
    values = jnp.clip(jax.random.normal(key, (PROMPTS, LP, KVH * HD), jnp.float32), -6.0, 6.0)
    return values.astype(jnp.bfloat16)


def steps_of(key, dims, split, low, top_value):
    loudness = 1.0
    for axis_at, shards_of in split:
        draws = jax.random.uniform(jax.random.fold_in(jax.random.fold_in(key, 6), axis_at), (shards_of,), jnp.float32, low / len(split), top_value / len(split))
        loudness = loudness * jnp.repeat(jnp.exp(draws), dims[axis_at] // shards_of).reshape((-1,) + (1,) * (len(dims) - 1 - axis_at))
    return loudness


def gaussian(own_key, extent, scale, limit, pieces=(), kind=jnp.bfloat16):
    array = scale * jax.random.normal(own_key, extent, jnp.float32)
    if pieces:
        array = array * steps_of(own_key, extent, pieces, -0.22, 0.18)
    return jnp.clip(array, -limit, limit).astype(kind)


def setup_inputs(seed: int = 0) -> dict:
    seeds = jax.random.split(jax.random.key(seed), 10)
    query = draw_query(jax.random.fold_in(seeds[9], 71), 0)
    comp_key = gaussian(seeds[1], (COMP, LC, KVH * HD), 1.0, 6.0, ((0, 64), (2, 8)))
    comp_value = gaussian(seeds[2], (COMP, LC, KVH * HD), 1.0, 6.0, ((0, 64), (2, 8)))
    prefix_key = draw_prefix_key(jax.random.fold_in(seeds[9], 71), 0)
    prefix_value = gaussian(seeds[4], (PROMPTS, LP, KVH * HD), 1.0, 6.0, ((0, 64), (1, 8)))
    grad_out = gaussian(seeds[5], (COMP, LC, QH * HD), 1.0, 6.0, ((0, 64), (2, 8)))
    owner = draw_owner(jax.random.fold_in(seeds[9], 71), 0)
    group = draw_group(jax.random.fold_in(seeds[9], 71), 0)
    lengths = draw_lengths(jax.random.fold_in(seeds[9], 71), 0)
    return dict(query=query, comp_key=comp_key, comp_value=comp_value, prefix_key=prefix_key, prefix_value=prefix_value, grad_out=grad_out, owner=owner, group=group, lengths=lengths)


def slot_grads(query, comp_key, comp_value, pre_key, pre_value, grad_out, length):
    row_count = query.shape[0]
    prefix_rows = pre_key.shape[0]
    kv_heads = comp_key.shape[1] // HD
    repeat = query.shape[1] // comp_key.shape[1]
    scaling = HD ** -0.5
    queries = query.astype(jnp.float32).reshape(row_count, kv_heads, repeat, HD)
    all_keys = jnp.concatenate([pre_key, comp_key], 0).astype(jnp.float32).reshape(prefix_rows + row_count, kv_heads, HD)
    all_values = jnp.concatenate([pre_value, comp_value], 0).astype(jnp.float32).reshape(prefix_rows + row_count, kv_heads, HD)
    scores = jnp.einsum("igrd,jgd->grij", queries, all_keys) * scaling
    query_pos = jnp.arange(row_count)[:, None]
    key_pos = jnp.arange(prefix_rows + row_count)[None, :]
    offset = key_pos - prefix_rows
    visible = (key_pos < prefix_rows) | ((offset <= query_pos) & (offset < length))
    scores = jnp.where(visible, scores, -jnp.inf)
    row_max = jnp.max(scores, axis=-1, keepdims=True)
    exponent = jnp.exp(scores - row_max)
    probability = exponent / jnp.sum(exponent, axis=-1, keepdims=True)
    weights = probability.astype(jnp.bfloat16).astype(jnp.float32)
    attended = jnp.einsum("grij,jgd->igrd", weights, all_values)
    live_rows = jnp.arange(row_count) < length
    upstream = jnp.where(live_rows[:, None], grad_out, jnp.zeros_like(grad_out))
    upstream = upstream.astype(jnp.float32).reshape(row_count, kv_heads, repeat, HD)
    grad_prob = jnp.einsum("igrd,jgd->grij", upstream, all_values)
    row_delta = jnp.transpose(jnp.sum(upstream * attended, axis=-1), (1, 2, 0))
    grad_score = (probability * (grad_prob - row_delta[..., None])).astype(jnp.bfloat16).astype(jnp.float32)
    grad_query = jnp.einsum("grij,jgd->igrd", grad_score, all_keys) * scaling
    grad_key = jnp.einsum("grij,igrd->jgd", grad_score, queries) * scaling
    grad_value = jnp.einsum("grij,igrd->jgd", weights, upstream)
    kv_width = kv_heads * HD
    grad_key = grad_key.reshape(prefix_rows + row_count, kv_width)
    grad_value = grad_value.reshape(prefix_rows + row_count, kv_width)
    return (grad_query.reshape(row_count, -1), grad_key[:prefix_rows], grad_value[:prefix_rows],
            grad_key[prefix_rows:], grad_value[prefix_rows:])


def reference(query, comp_key, comp_value, prefix_key, prefix_value, grad_out, owner, group, lengths):
    empty = jnp.zeros(prefix_key.shape, jnp.float32)

    def advance(carry, inputs):
        key_total, value_total = carry
        one_query, one_key, one_value, one_grad, prompt, length = inputs
        holder = owner[prompt].astype(jnp.int32)
        pre_key = lax.dynamic_index_in_dim(prefix_key, holder, 0, keepdims=False)
        pre_value = lax.dynamic_index_in_dim(prefix_value, holder, 0, keepdims=False)
        grad_q, key_pre, value_pre, key_comp, value_comp = slot_grads(
            one_query, one_key, one_value, pre_key, pre_value, one_grad, length)
        key_total = key_total.at[holder].add(key_pre)
        value_total = value_total.at[holder].add(value_pre)
        return (key_total, value_total), (grad_q.astype(jnp.bfloat16), key_comp.astype(jnp.bfloat16),
                                          value_comp.astype(jnp.bfloat16))

    (key_total, value_total), (grad_q, key_comp, value_comp) = lax.scan(
        advance, (empty, empty), (query, comp_key, comp_value, grad_out, group, lengths))
    return grad_q, key_comp, value_comp, key_total.astype(jnp.bfloat16), value_total.astype(jnp.bfloat16)
```

```python
import functools

import jax
import jax.numpy as jnp
from jax import lax
from jax.experimental import pallas as pl
from jax.experimental.pallas import tpu as pltpu
from jax.sharding import PartitionSpec as P

HD = 128
SCALE = HD**-0.5
LOG2E = 1.4426950408889634
CHUNK = 128
HALF = 16
HIDDEN = -1e30
NT = (((1,), (1,)), ((), ()))


def dot(left, right):
    return jnp.dot(left, right, preferred_element_type=jnp.float32)


def dot_nt(left, right):
    return lax.dot_general(left, right, NT, preferred_element_type=jnp.float32)


def fold(value, reduce):
    return reduce(value.reshape(-1, 8, value.shape[-1]), axis=0)


def block_rows(ref, slot, half):
    heads = ref.shape[2] // HD
    rows = pl.ds(pl.multiple_of(half * HALF, HALF), HALF)
    return jnp.concatenate(
        [ref[slot, rows, head * HD : (head + 1) * HD] for head in range(heads)], axis=0
    )


def live_rows(block, half, length):
    row = lax.broadcasted_iota(jnp.int32, block.shape, 0) % HALF + half * HALF
    return jnp.where(row < length, block.astype(jnp.float32), 0.0).astype(jnp.bfloat16)


def two_blocks(
    first, second, lengths, query, comp_key, comp_value, grad_out, dq_buf, dk_sum, dv_sum,
    keys, values, key_flip, weight_buf, slope_buf, exp_buf, prob_buf, key_sum, value_sum
):
    slots = query.shape[1]
    prefix = key_sum.shape[0]
    extent = keys.shape[0]
    blocks = (first, second)
    spots = [(slot, half, jnp.where(valid, lengths[slot], 0)) for slot, half, valid in blocks]
    queries = jnp.concatenate([block_rows(query, slot, half) for slot, half, _ in spots], axis=0)
    upstream = jnp.concatenate(
        [live_rows(block_rows(grad_out, slot, half), half, size) for slot, half, size in spots],
        axis=0,
    )
    lanes = queries.shape[0]
    for at, (slot, _, _) in enumerate(spots):
        keys[prefix + at * slots : prefix + (at + 1) * slots] = comp_key[slot]
        values[prefix + at * slots : prefix + (at + 1) * slots] = comp_value[slot]

    row = lax.broadcasted_iota(jnp.int32, (2 * slots, lanes), 0)
    lane = lax.broadcasted_iota(jnp.int32, (2 * slots, lanes), 1)
    side = lane // (lanes // 2)
    key_at = row % slots
    query_at = lane % HALF + HALF * jnp.where(side == 0, spots[0][1], spots[1][1])
    size = jnp.where(side == 0, spots[0][2], spots[1][2])
    visible = (row // slots == side) & (key_at <= query_at) & (key_at < size)

    spans = [(start, min(start + CHUNK, extent)) for start in range(0, extent, CHUNK)]
    scores = dot_nt(keys[...], queries)
    slope_buf[...] = dot_nt(values[...], upstream)
    tops, sums = [], []
    for start, end in spans:
        part = scores[start:end]
        if start >= prefix:
            part = jnp.where(visible, part, HIDDEN)
        top = jnp.max(fold(part, jnp.max), axis=0, keepdims=True)
        part = jnp.exp2((part - top) * (SCALE * LOG2E))
        exp_buf[start:end] = part
        tops.append(top)
        sums.append(fold(part, jnp.sum))
    top = functools.reduce(jnp.maximum, tops)
    shares = [jnp.exp2((each - top) * (SCALE * LOG2E)) for each in tops]
    total = sum(part * share for part, share in zip(sums, shares))
    inverse = 1.0 / jnp.sum(total, axis=0, keepdims=True)
    shares = [share * inverse for share in shares]

    delta = 0.0
    for (start, end), share in zip(spans, shares):
        weight = (exp_buf[start:end] * share).astype(jnp.bfloat16)
        weight_buf[start:end] = weight
        delta = delta + fold(weight.astype(jnp.float32) * slope_buf[start:end], jnp.sum)
    delta = jnp.sum(delta, axis=0, keepdims=True)
    terms = dot(weight_buf[...], upstream)
    value_sum[...] += terms[:prefix]
    for at, (slot, _, _) in enumerate(spots):
        dv_sum[slot] += terms[prefix + at * slots : prefix + (at + 1) * slots]

    for (start, end), share in zip(spans, shares):
        part = exp_buf[start:end] * share * (slope_buf[start:end] - delta)
        prob_buf[start:end] = part.astype(jnp.bfloat16)
    terms = dot(prob_buf[...], queries)
    key_sum[...] += terms[:prefix]
    for at, (slot, _, _) in enumerate(spots):
        dk_sum[slot] += terms[prefix + at * slots : prefix + (at + 1) * slots]
    own_flip = keys[prefix:].astype(jnp.float32).T.astype(jnp.bfloat16)
    flipped = dot(key_flip[...], prob_buf[:prefix]) + dot(own_flip, prob_buf[prefix:])
    query_grad = (flipped.T * SCALE).astype(jnp.bfloat16)
    for at, (slot, half, valid) in enumerate(blocks):

        @pl.when(valid)
        def _():
            rows = pl.ds(pl.multiple_of(half * HALF, HALF), HALF)
            for head in range(query.shape[2] // HD):
                start = at * (lanes // 2) + head * HALF
                dq_buf[slot, rows, head * HD : (head + 1) * HD] = query_grad[start : start + HALF]


def near_kernel(
    code, chained, near, lengths, query, comp_key, comp_value, grad_out, pair, *refs
):
    if chained:
        refs = refs[3:]
    (term, dq, dk, dv, dq_buf, dk_buf, dv_buf, dk_sum, dv_sum, keys, values, key_flip,
     weight_buf, slope_buf, exp_buf, prob_buf, key_sum, value_sum, listed, out_sem) = refs
    count = near.shape[0]
    prefix = key_sum.shape[0]
    rows = pair.shape[2]

    def stores(slot):
        return [
            pltpu.make_async_copy(source.at[slot], target.at[slot], out_sem.at[at, slot])
            for at, (source, target) in enumerate(((dq_buf, dq), (dk_buf, dk), (dv_buf, dv)))
        ]

    def gather(slot, found):
        @pl.when(near[slot] == code)
        def _():
            listed[found] = 2 * slot
            listed[found + 1] = 2 * slot + 1
            dk_sum[slot] = jnp.zeros_like(dk_sum[slot])
            dv_sum[slot] = jnp.zeros_like(dv_sum[slot])

        blocks = jnp.where(lengths[slot] > HALF, 2, 1)
        return found + jnp.where(near[slot] == code, blocks, 0)

    found = lax.fori_loop(0, count, gather, 0)
    key_sum[...] = jnp.zeros_like(key_sum)
    value_sum[...] = jnp.zeros_like(value_sum)

    @pl.when(found > 0)
    def _():
        for at in range(pair.shape[0]):
            span = slice(at * rows, (at + 1) * rows)
            keys[span] = pair[at, 0]
            values[span] = pair[at, 1]
            key_flip[:, span] = pair[at, 0].astype(jnp.float32).T.astype(jnp.bfloat16)

    def step(at, carry):
        def spot(index):
            return listed[index] // 2, listed[index] % 2

        one_slot, one_half = spot(2 * at)
        valid = 2 * at + 1 < found
        two_slot, two_half = spot(jnp.where(valid, 2 * at + 1, 2 * at))
        two_blocks(
            (one_slot, one_half, 2 * at < found), (two_slot, two_half, valid), lengths,
            query, comp_key, comp_value, grad_out, dq_buf, dk_sum, dv_sum, keys, values,
            key_flip, weight_buf, slope_buf, exp_buf, prob_buf, key_sum, value_sum
        )
        return carry

    lax.fori_loop(0, (found + 1) // 2, step, 0)

    def send(slot, carry):
        @pl.when(near[slot] == code)
        def _():
            @pl.when(lengths[slot] <= HALF)
            def _():
                dq_buf[slot, HALF:] = jnp.zeros_like(dq_buf[slot, HALF:])

            dk_buf[slot] = (dk_sum[slot] * SCALE).astype(jnp.bfloat16)
            dv_buf[slot] = dv_sum[slot].astype(jnp.bfloat16)
            for copy in stores(slot):
                copy.start()

        return carry

    def finish(slot, carry):
        @pl.when(near[slot] == code)
        def _():
            for copy in stores(slot):
                copy.wait()

        return carry

    lax.fori_loop(0, count, send, 0)
    for at in range(pair.shape[0]):
        span = slice(at * rows, (at + 1) * rows)
        term[at, 0] = (key_sum[span] * SCALE).astype(term.dtype)
        term[at, 1] = value_sum[span].astype(term.dtype)
    lax.fori_loop(0, count, finish, 0)


def near_grads(code, pair, near, lengths, query, comp_key, comp_value, grad_out, chain, kind):
    count, slots, width = query.shape
    lanes = 2 * HALF * (width // HD)
    prefix = pair.shape[0] * pair.shape[2]
    extent = prefix + 2 * slots
    anywhere = pl.BlockSpec(memory_space=pl.ANY)
    scalar = pl.BlockSpec(memory_space=pltpu.SMEM)
    vmem = pl.BlockSpec(memory_space=pltpu.VMEM)
    narrow = jax.ShapeDtypeStruct(comp_key.shape, jnp.bfloat16)
    operands = [near, lengths, query, comp_key, comp_value, grad_out, pair]
    aliases = {}
    if chain is not None:
        aliases = {len(operands) + at: 1 + at for at in range(3)}
        operands += list(chain)
    work = 4
    out = pl.pallas_call(
        functools.partial(near_kernel, code, chain is not None),
        out_shape=[
            jax.ShapeDtypeStruct(pair.shape, kind),
            jax.ShapeDtypeStruct(query.shape, jnp.bfloat16),
            narrow,
            narrow,
        ],
        in_specs=[scalar] * 2 + [vmem] * 5 + [anywhere] * len(aliases),
        out_specs=[vmem] + [anywhere] * 3,
        scratch_shapes=[
            pltpu.VMEM(query.shape, jnp.bfloat16),
            pltpu.VMEM(comp_key.shape, jnp.bfloat16),
            pltpu.VMEM(comp_key.shape, jnp.bfloat16),
            pltpu.VMEM(comp_key.shape, jnp.float32),
            pltpu.VMEM(comp_key.shape, jnp.float32),
            pltpu.VMEM((extent, HD), jnp.bfloat16),
            pltpu.VMEM((extent, HD), jnp.bfloat16),
            pltpu.VMEM((HD, prefix), jnp.bfloat16),
            pltpu.VMEM((extent, lanes), jnp.bfloat16),
            pltpu.VMEM((extent, lanes), jnp.float32),
            pltpu.VMEM((extent, lanes), jnp.float32),
            pltpu.VMEM((extent, lanes), jnp.bfloat16),
            pltpu.VMEM((prefix, HD), jnp.float32),
            pltpu.VMEM((prefix, HD), jnp.float32),
            pltpu.SMEM((2 * count + 2,), jnp.int32),
            pltpu.SemaphoreType.DMA((3, count)),
        ],
        input_output_aliases=aliases,
        compiler_params=pltpu.CompilerParams(vmem_limit_bytes=28 * 2**20),
        cost_estimate=pl.CostEstimate(
            flops=work * 12 * extent * lanes * HD,
            bytes_accessed=work * 10 * slots * width,
            transcendentals=work * extent * lanes,
        ),
    )(*operands)
    return out[0], out[1:]


def split_kernel(key, value, pair):
    for head in range(pair.shape[0]):
        columns = slice(head * HD, (head + 1) * HD)
        pair[head, 0] = key[:, columns]
        pair[head, 1] = value[:, columns]


def split_heads(key, value, shards):
    return pl.pallas_call(
        split_kernel,
        out_shape=jax.ShapeDtypeStruct((shards, 2, key.shape[0], HD), key.dtype),
    )(key, value)


def join_kernel(pair, key, value):
    for head in range(pair.shape[0]):
        columns = slice(head * HD, (head + 1) * HD)
        key[:, columns] = pair[head, 0]
        value[:, columns] = pair[head, 1]


def join_heads(pair):
    shards, _, rows, _ = pair.shape
    whole = jax.ShapeDtypeStruct((rows, shards * HD), pair.dtype)
    return pl.pallas_call(join_kernel, out_shape=[whole, whole])(pair)


def shifted(value, steps):
    size, shards = lax.axis_size("dp"), lax.axis_size("mp")
    pairs = []
    for at in range(size):
        for shard in range(shards):
            target = (at + (steps if shard % 2 == 0 else -steps)) % size
            pairs.append((at * shards + shard, target * shards + shard))
    return lax.ppermute(value, ("dp", "mp"), pairs)


def per_device(
    query, comp_key, comp_value, prefix_key, prefix_value, grad_out, owner, group, lengths
):
    axis_count = lax.axis_size("dp")
    shards = lax.axis_size("mp")
    position = lax.axis_index("dp")
    prompt_ids = jnp.arange(owner.shape[0], dtype=jnp.int32)
    holder_of = jnp.sum(jnp.where(group[:, None] == prompt_ids[None, :], owner[None, :], 0), axis=1)
    near = ((holder_of - position + 2 + axis_count) % axis_count).astype(jnp.int32)
    near = jnp.where(lax.axis_index("mp") % 2 == 0, near, 4 - near)

    pair = split_heads(prefix_key[0], prefix_value[0], shards)
    own = lax.all_to_all(pair, "mp", split_axis=0, concat_axis=0, tiled=True)
    low_one = shifted(own, 1)
    up_one = shifted(own, -1)
    low_two = shifted(low_one, 1)
    up_two = shifted(up_one, -1)

    arrays = (near, lengths, query, comp_key, comp_value, grad_out)
    own_term, chain = near_grads(2, own, *arrays, None, jnp.float32)
    low_two_term, chain = near_grads(0, low_two, *arrays, chain, jnp.bfloat16)
    up_two_term, chain = near_grads(4, up_two, *arrays, chain, jnp.bfloat16)
    low_term, chain = near_grads(1, low_one, *arrays, chain, jnp.float32)
    up_term, chain = near_grads(3, up_one, *arrays, chain, jnp.float32)
    low_back = shifted(low_two_term, -1).astype(jnp.float32)
    up_back = shifted(up_two_term, 1).astype(jnp.float32)
    low_back = shifted((low_term + low_back).astype(jnp.bfloat16), -1).astype(jnp.float32)
    up_back = shifted((up_term + up_back).astype(jnp.bfloat16), 1).astype(jnp.float32)
    gathered = (own_term + low_back + up_back).astype(jnp.bfloat16)
    back = lax.all_to_all(gathered, "mp", split_axis=0, concat_axis=0, tiled=True)
    key_back, value_back = join_heads(back)
    return chain[0], chain[1], chain[2], key_back[None], value_back[None]


def solution(mesh):
    return jax.shard_map(
        per_device,
        mesh=mesh,
        in_specs=(
            P("dp", None, "mp"),
            P("dp", None, "mp"),
            P("dp", None, "mp"),
            P("dp", "mp", None),
            P("dp", "mp", None),
            P("dp", None, "mp"),
            P(),
            P("dp"),
            P("dp"),
        ),
        out_specs=(
            P("dp", None, "mp"),
            P("dp", None, "mp"),
            P("dp", None, "mp"),
            P("dp", "mp", None),
            P("dp", "mp", None),
        ),
        check_vma=False,
    )
```

```python
import functools

import jax
import jax.numpy as jnp
from jax import lax
from jax.experimental import pallas as pl
from jax.experimental.pallas import tpu as pltpu
from jax.sharding import PartitionSpec as P

HD = 128
SCALE = HD**-0.5
LOG2E = 1.4426950408889634
CHUNK = 128
HALF = 16
HIDDEN = -1e30


def dot(left, right):
    return jnp.dot(left, right, preferred_element_type=jnp.float32)


def fold(value, reduce):
    return reduce(value.reshape(-1, 8, value.shape[-1]), axis=0)


def prepare_kernel(lengths, query, grad_out, query_rows, query_flip, live, live_flip):
    slots = query.shape[1]
    heads = query.shape[2] // HD
    for ref in (query_rows, query_flip, live, live_flip):
        ref[ref.shape[0] - 1] = jnp.zeros_like(ref[0])

    def step(slot, carry):
        for half in range(slots // HALF):
            rows = slice(half * HALF, (half + 1) * HALF)
            cells = [(rows, slice(head * HD, (head + 1) * HD)) for head in range(heads)]
            at = slot * (slots // HALF) + half
            block = jnp.concatenate([query[slot, row, col] for row, col in cells], axis=0)
            query_rows[at] = block
            query_flip[at] = block.T
            row_at = lax.broadcasted_iota(jnp.int32, (HALF, HD), 0) + half * HALF
            block = jnp.concatenate(
                [
                    jnp.where(
                        row_at < lengths[slot], grad_out[slot, row, col].astype(jnp.float32), 0.0
                    ).astype(jnp.bfloat16)
                    for row, col in cells
                ],
                axis=0,
            )
            live[at] = block
            live_flip[at] = block.T
        return carry

    lax.fori_loop(0, query.shape[0], step, 0)


def prepare(lengths, query, grad_out):
    count, slots, width = query.shape
    blocks = count * (slots // HALF) + 1
    rows = HALF * (width // HD)
    vmem = pl.BlockSpec(memory_space=pltpu.VMEM)
    tall = jax.ShapeDtypeStruct((blocks, rows, HD), jnp.bfloat16)
    wide = jax.ShapeDtypeStruct((blocks, HD, rows), jnp.bfloat16)
    return pl.pallas_call(
        prepare_kernel,
        out_shape=[tall, wide, tall, wide],
        in_specs=[pl.BlockSpec(memory_space=pltpu.SMEM), vmem, vmem],
        out_specs=[vmem] * 4,
        compiler_params=pltpu.CompilerParams(vmem_limit_bytes=8 * 2**20),
        cost_estimate=pl.CostEstimate(
            flops=0, bytes_accessed=12 * count * slots * width, transcendentals=0
        ),
    )(lengths, query, grad_out)


def stack(ref, spots, axis):
    return jnp.concatenate([ref[block] for block, _, _, _ in spots], axis=axis)


def first_half(spots, prepared, comp_key, comp_value, prefix, bufs):
    _, query_flip, _, live_flip = prepared
    keys, values, _, slope_buf, exp_buf, _ = bufs
    slots = comp_key.shape[1]
    extent = keys.shape[0]
    for at, (_, slot, _, _) in enumerate(spots):
        keys[prefix + at * slots : prefix + (at + 1) * slots] = comp_key[slot]
        values[prefix + at * slots : prefix + (at + 1) * slots] = comp_value[slot]
    queries = stack(query_flip, spots, 1)
    lanes = queries.shape[1]
    row = lax.broadcasted_iota(jnp.int32, (2 * slots, lanes), 0)
    lane = lax.broadcasted_iota(jnp.int32, (2 * slots, lanes), 1)
    side = lane // (lanes // 2)
    key_at = row % slots
    query_at = lane % HALF + HALF * jnp.where(side == 0, spots[0][2], spots[1][2])
    size = jnp.where(side == 0, spots[0][3], spots[1][3])
    visible = (row // slots == side) & (key_at <= query_at) & (key_at < size)

    spans = [(start, min(start + CHUNK, extent)) for start in range(0, extent, CHUNK)]
    scores = dot(keys[...], queries)
    slope_buf[...] = dot(values[...], stack(live_flip, spots, 1))
    tops, sums = [], []
    for start, end in spans:
        part = scores[start:end]
        if start >= prefix:
            part = jnp.where(visible, part, HIDDEN)
        top = jnp.max(fold(part, jnp.max), axis=0, keepdims=True)
        part = jnp.exp2((part - top) * (SCALE * LOG2E))
        exp_buf[start:end] = part
        tops.append(top)
        sums.append(fold(part, jnp.sum))
    top = functools.reduce(jnp.maximum, tops)
    shares = [jnp.exp2((each - top) * (SCALE * LOG2E)) for each in tops]
    total = sum(part * share for part, share in zip(sums, shares))
    inverse = 1.0 / jnp.sum(total, axis=0, keepdims=True)
    return spans, [share * inverse for share in shares]


def second_half(state, spots, prepared, key_flip, bufs, prefix, dk_sum, dv_sum, dq):
    query_rows, _, live, _ = prepared
    keys, _, weight_buf, slope_buf, exp_buf, prob_buf = bufs
    slots = dk_sum.shape[1]
    spans, shares = state
    delta = 0.0
    for (start, end), share in zip(spans, shares):
        weight = (exp_buf[start:end] * share).astype(jnp.bfloat16)
        weight_buf[start:end] = weight
        delta = delta + fold(weight.astype(jnp.float32) * slope_buf[start:end], jnp.sum)
    delta = jnp.sum(delta, axis=0, keepdims=True)
    value_terms = dot(weight_buf[...], stack(live, spots, 0))
    for (start, end), share in zip(spans, shares):
        part = exp_buf[start:end] * share * (slope_buf[start:end] - delta)
        prob_buf[start:end] = part.astype(jnp.bfloat16)
    key_terms = dot(prob_buf[...], stack(query_rows, spots, 0)) * SCALE
    own_flip = keys[prefix:].astype(jnp.float32).T.astype(jnp.bfloat16)
    flipped = dot(key_flip[...], prob_buf[:prefix]) + dot(own_flip, prob_buf[prefix:])
    query_grad = (flipped * SCALE).T.astype(jnp.bfloat16)
    for at, (_, slot, _, _) in enumerate(spots):
        span = slice(prefix + at * slots, prefix + (at + 1) * slots)
        dv_sum[slot] += value_terms[span]
        dk_sum[slot] += key_terms[span]
    return key_terms[:prefix], value_terms[:prefix], query_grad


def put_query_grad(dq, spots, query_grad):
    half_rows = query_grad.shape[0] // 2
    for at, (block, slot, half, _) in enumerate(spots):

        def put():
            rows = pl.ds(pl.multiple_of(half * HALF, HALF), HALF)
            for head in range(dq.shape[2] // HD):
                start = at * half_rows + head * HALF
                dq[slot, rows, head * HD : (head + 1) * HD] = query_grad[start : start + HALF]

        if at == 0:
            put()
        else:
            pl.when(block < 2 * dq.shape[0])(put)


def near_kernel(code, chained, plan, query_rows, query_flip, live, live_flip, comp_key, comp_value,
                pair, *refs):
    if chained:
        for done, out in zip(refs[:3], refs[4:7]):
            out[...] = done[...]
        refs = refs[3:]
    (term, dq, dk, dv, dk_sum, dv_sum, key_flip, key_sum, value_sum, listed) = refs[:10]
    bufs = (refs[10:16], refs[16:22])
    count, slots = dq.shape[:2]
    prefix = key_sum.shape[0]
    rows = pair.shape[2]
    prepared = (query_rows, query_flip, live, live_flip)

    def size_of(slot):
        return plan[slot] % 64

    found = 0
    for slot in range(count):
        word = plan[slot]
        listed[found] = 2 * slot
        listed[found + 1] = 2 * slot + 1
        blocks = jnp.where(word % 64 > HALF, 2, 1)
        found = found + jnp.where(word // 64 == code, blocks, 0)
    key_sum[...] = jnp.zeros_like(key_sum)
    value_sum[...] = jnp.zeros_like(value_sum)

    @pl.when(found > 0)
    def _():
        dk_sum[...] = jnp.zeros_like(dk_sum)
        dv_sum[...] = jnp.zeros_like(dv_sum)
        for at in range(pair.shape[0]):
            span = slice(at * rows, (at + 1) * rows)
            for keys, values, *_ in bufs:
                keys[span] = pair[at, 0]
                values[span] = pair[at, 1]
            key_flip[:, span] = pair[at, 0].T

    def spots_at(index):
        one = listed[index]
        other = listed[index + 1]
        valid = index + 1 < found
        slot = jnp.where(valid, other // 2, one // 2)
        return (
            (one, one // 2, one % 2, size_of(one // 2)),
            (jnp.where(valid, other, 2 * count), slot, jnp.where(valid, other % 2, 0),
             jnp.where(valid, size_of(slot), 0)),
        )

    def run(starts):
        all_spots = [spots_at(start) for start in starts]
        states = [
            first_half(spots, prepared, comp_key, comp_value, prefix, buf)
            for spots, buf in zip(all_spots, bufs)
        ]
        done = [
            second_half(state, spots, prepared, key_flip, buf, prefix, dk_sum, dv_sum, dq)
            for state, spots, buf in zip(states, all_spots, bufs)
        ]
        key_sum[...] += sum(each[0] for each in done)
        value_sum[...] += sum(each[1] for each in done)
        for spots, each in zip(all_spots, done):
            put_query_grad(dq, spots, each[2])

    pairs = (found + 1) // 2

    def step(at, carry):
        run((4 * at, 4 * at + 2))
        return carry

    lax.fori_loop(0, pairs // 2, step, 0)

    @pl.when(pairs % 2 == 1)
    def _():
        run((2 * pairs - 2,))

    def finish(index, carry):
        block = listed[index]
        slot = block // 2

        @pl.when(block % 2 == 0)
        def _():
            dk[slot] = dk_sum[slot].astype(jnp.bfloat16)
            dv[slot] = dv_sum[slot].astype(jnp.bfloat16)

            @pl.when(size_of(slot) <= HALF)
            def _():
                dq[slot, HALF:] = jnp.zeros_like(dq[slot, HALF:])

        return carry

    lax.fori_loop(0, found, finish, 0)
    for at in range(pair.shape[0]):
        span = slice(at * rows, (at + 1) * rows)
        term[at, 0] = key_sum[span].astype(term.dtype)
        term[at, 1] = value_sum[span].astype(term.dtype)


def near_grads(code, pair, plan, prepared, comp_key, comp_value, chain, shape, kind):
    count, slots, width = shape
    lanes = 2 * HALF * (width // HD)
    prefix = pair.shape[0] * pair.shape[2]
    extent = prefix + 2 * slots
    vmem = pl.BlockSpec(memory_space=pltpu.VMEM)
    narrow = jax.ShapeDtypeStruct(comp_key.shape, jnp.bfloat16)
    operands = [plan, *prepared, comp_key, comp_value, pair]
    if chain is not None:
        operands += list(chain)
    work = 4
    out = pl.pallas_call(
        functools.partial(near_kernel, code, chain is not None),
        out_shape=[
            jax.ShapeDtypeStruct(pair.shape, kind),
            jax.ShapeDtypeStruct(shape, jnp.bfloat16),
            narrow,
            narrow,
        ],
        in_specs=[pl.BlockSpec(memory_space=pltpu.SMEM)] + [vmem] * (len(operands) - 1),
        out_specs=[vmem] * 4,
        scratch_shapes=[
            pltpu.VMEM(comp_key.shape, jnp.float32),
            pltpu.VMEM(comp_key.shape, jnp.float32),
            pltpu.VMEM((HD, prefix), jnp.bfloat16),
            pltpu.VMEM((prefix, HD), jnp.float32),
            pltpu.VMEM((prefix, HD), jnp.float32),
            pltpu.SMEM((2 * count + 4,), jnp.int32),
        ]
        + 2
        * [
            pltpu.VMEM((extent, HD), jnp.bfloat16),
            pltpu.VMEM((extent, HD), jnp.bfloat16),
            pltpu.VMEM((extent, lanes), jnp.bfloat16),
            pltpu.VMEM((extent, lanes), jnp.float32),
            pltpu.VMEM((extent, lanes), jnp.float32),
            pltpu.VMEM((extent, lanes), jnp.bfloat16),
        ],
        compiler_params=pltpu.CompilerParams(vmem_limit_bytes=24 * 2**20),
        cost_estimate=pl.CostEstimate(
            flops=work * 12 * extent * lanes * HD,
            bytes_accessed=work * 10 * slots * width,
            transcendentals=work * extent * lanes,
        ),
    )(*operands)
    return out[0], out[1:]


SMALL = pltpu.CompilerParams(vmem_limit_bytes=4 * 2**20)


def split_kernel(key, value, pair):
    for head in range(pair.shape[0]):
        columns = slice(head * HD, (head + 1) * HD)
        pair[head, 0] = key[:, columns]
        pair[head, 1] = value[:, columns]


def split_heads(key, value, shards):
    return pl.pallas_call(
        split_kernel,
        out_shape=jax.ShapeDtypeStruct((shards, 2, key.shape[0], HD), key.dtype),
        compiler_params=SMALL,
    )(key, value)


def join_kernel(pair, key, value):
    for head in range(pair.shape[0]):
        columns = slice(head * HD, (head + 1) * HD)
        key[:, columns] = pair[head, 0]
        value[:, columns] = pair[head, 1]


def join_heads(pair):
    shards, _, rows, _ = pair.shape
    whole = jax.ShapeDtypeStruct((rows, shards * HD), pair.dtype)
    return pl.pallas_call(join_kernel, out_shape=[whole, whole], compiler_params=SMALL)(pair)


def shifted(value, steps):
    size, shards = lax.axis_size("dp"), lax.axis_size("mp")
    pairs = []
    for at in range(size):
        for shard in range(shards):
            target = (at + (steps if shard % 2 == 0 else -steps)) % size
            pairs.append((at * shards + shard, target * shards + shard))
    return lax.ppermute(value, ("dp", "mp"), pairs)


def per_device(
    query, comp_key, comp_value, prefix_key, prefix_value, grad_out, owner, group, lengths
):
    axis_count = lax.axis_size("dp")
    shards = lax.axis_size("mp")
    position = lax.axis_index("dp")
    prompt_ids = jnp.arange(owner.shape[0], dtype=jnp.int32)
    holder_of = jnp.sum(jnp.where(group[:, None] == prompt_ids[None, :], owner[None, :], 0), axis=1)
    near = ((holder_of - position + 2 + axis_count) % axis_count).astype(jnp.int32)
    near = jnp.where(lax.axis_index("mp") % 2 == 0, near, 4 - near)

    pair = split_heads(prefix_key[0], prefix_value[0], shards)
    own = lax.all_to_all(pair, "mp", split_axis=0, concat_axis=0, tiled=True)
    low_one = shifted(own, 1)
    up_one = shifted(own, -1)
    low_two = shifted(low_one, 1)
    up_two = shifted(up_one, -1)

    plan = near * 64 + lengths
    prepared = prepare(lengths, query, grad_out)
    rest = (comp_key, comp_value)
    own_term, chain = near_grads(2, own, plan, prepared, *rest, None, query.shape, jnp.float32)
    low_two_term, chain = near_grads(0, low_two, plan, prepared, *rest, chain, query.shape, jnp.bfloat16)
    up_two_term, chain = near_grads(4, up_two, plan, prepared, *rest, chain, query.shape, jnp.bfloat16)
    low_term, chain = near_grads(1, low_one, plan, prepared, *rest, chain, query.shape, jnp.float32)
    up_term, chain = near_grads(3, up_one, plan, prepared, *rest, chain, query.shape, jnp.float32)
    low_back = shifted(low_two_term, -1).astype(jnp.float32)
    up_back = shifted(up_two_term, 1).astype(jnp.float32)
    low_back = shifted((low_term + low_back).astype(jnp.bfloat16), -1).astype(jnp.float32)
    up_back = shifted((up_term + up_back).astype(jnp.bfloat16), 1).astype(jnp.float32)
    gathered = (own_term + low_back + up_back).astype(jnp.bfloat16)
    back = lax.all_to_all(gathered, "mp", split_axis=0, concat_axis=0, tiled=True)
    key_back, value_back = join_heads(back)
    return chain[0], chain[1], chain[2], key_back[None], value_back[None]


def solution(mesh):
    return jax.shard_map(
        per_device,
        mesh=mesh,
        in_specs=(
            P("dp", None, "mp"),
            P("dp", None, "mp"),
            P("dp", None, "mp"),
            P("dp", "mp", None),
            P("dp", "mp", None),
            P("dp", None, "mp"),
            P(),
            P("dp"),
            P("dp"),
        ),
        out_specs=(
            P("dp", None, "mp"),
            P("dp", None, "mp"),
            P("dp", None, "mp"),
            P("dp", "mp", None),
            P("dp", "mp", None),
        ),
        check_vma=False,
    )
```

```python
import functools

import jax
import jax.numpy as jnp
from jax import lax
from jax.experimental import pallas as pl
from jax.experimental.pallas import tpu as pltpu
from jax.sharding import PartitionSpec as P

HD = 128
SCALE = HD**-0.5
LOG2E = 1.4426950408889634
CHUNK = 128
HALF = 16
HIDDEN = -1e30


def dot(left, right):
    return jnp.dot(left, right, preferred_element_type=jnp.float32)


def fold(value, reduce):
    return reduce(value.reshape(-1, 8, value.shape[-1]), axis=0)


def prepare_kernel(lengths, query, grad_out, query_rows, query_flip, live, live_flip):
    slots = query.shape[1]
    heads = query.shape[2] // HD
    for ref in (query_rows, query_flip, live, live_flip):
        ref[ref.shape[0] - 1] = jnp.zeros_like(ref[0])

    def step(slot, carry):
        for half in range(slots // HALF):
            rows = slice(half * HALF, (half + 1) * HALF)
            cells = [(rows, slice(head * HD, (head + 1) * HD)) for head in range(heads)]
            at = slot * (slots // HALF) + half
            block = jnp.concatenate([query[slot, row, col] for row, col in cells], axis=0)
            query_rows[at] = block
            query_flip[at] = block.T
            row_at = lax.broadcasted_iota(jnp.int32, (HALF, HD), 0) + half * HALF
            block = jnp.concatenate(
                [
                    jnp.where(
                        row_at < lengths[slot], grad_out[slot, row, col].astype(jnp.float32), 0.0
                    ).astype(jnp.bfloat16)
                    for row, col in cells
                ],
                axis=0,
            )
            live[at] = block
            live_flip[at] = block.T
        return carry

    lax.fori_loop(0, query.shape[0], step, 0)


def prepare(lengths, query, grad_out):
    count, slots, width = query.shape
    blocks = count * (slots // HALF) + 1
    rows = HALF * (width // HD)
    vmem = pl.BlockSpec(memory_space=pltpu.VMEM)
    tall = jax.ShapeDtypeStruct((blocks, rows, HD), jnp.bfloat16)
    wide = jax.ShapeDtypeStruct((blocks, HD, rows), jnp.bfloat16)
    return pl.pallas_call(
        prepare_kernel,
        out_shape=[tall, wide, tall, wide],
        in_specs=[pl.BlockSpec(memory_space=pltpu.SMEM), vmem, vmem],
        out_specs=[vmem] * 4,
        compiler_params=pltpu.CompilerParams(vmem_limit_bytes=8 * 2**20),
        cost_estimate=pl.CostEstimate(
            flops=0, bytes_accessed=12 * count * slots * width, transcendentals=0
        ),
    )(lengths, query, grad_out)


def stack(ref, spots, axis):
    return jnp.concatenate([ref[block] for block, _, _, _ in spots], axis=axis)


def first_half(spots, prepared, comp_key, comp_value, prefix, bufs):
    _, query_flip, _, live_flip = prepared
    keys, values, _, slope_buf, exp_buf, _ = bufs
    slots = comp_key.shape[1]
    extent = keys.shape[0]
    for at, (_, slot, _, _) in enumerate(spots):
        keys[prefix + at * slots : prefix + (at + 1) * slots] = comp_key[slot]
        values[prefix + at * slots : prefix + (at + 1) * slots] = comp_value[slot]
    queries = stack(query_flip, spots, 1)
    lanes = queries.shape[1]
    row = lax.broadcasted_iota(jnp.int32, (2 * slots, lanes), 0)
    lane = lax.broadcasted_iota(jnp.int32, (2 * slots, lanes), 1)
    side = lane // (lanes // 2)
    key_at = row % slots
    query_at = lane % HALF + HALF * jnp.where(side == 0, spots[0][2], spots[1][2])
    size = jnp.where(side == 0, spots[0][3], spots[1][3])
    visible = (row // slots == side) & (key_at <= query_at) & (key_at < size)

    spans = [(start, min(start + CHUNK, extent)) for start in range(0, extent, CHUNK)]
    scores = dot(keys[...], queries)
    slope_buf[...] = dot(values[...], stack(live_flip, spots, 1))
    tops, sums = [], []
    for start, end in spans:
        part = scores[start:end]
        if start >= prefix:
            part = jnp.where(visible, part, HIDDEN)
        top = jnp.max(fold(part, jnp.max), axis=0, keepdims=True)
        part = jnp.exp2((part - top) * (SCALE * LOG2E))
        exp_buf[start:end] = part
        tops.append(top)
        sums.append(fold(part, jnp.sum))
    top = functools.reduce(jnp.maximum, tops)
    shares = [jnp.exp2((each - top) * (SCALE * LOG2E)) for each in tops]
    total = sum(part * share for part, share in zip(sums, shares))
    inverse = 1.0 / jnp.sum(total, axis=0, keepdims=True)
    return spans, [share * inverse for share in shares]


def second_half(state, spots, prepared, key_flip, bufs, prefix, dk_sum, dv_sum, dq):
    query_rows, _, live, _ = prepared
    keys, _, weight_buf, slope_buf, exp_buf, prob_buf = bufs
    slots = dk_sum.shape[1]
    spans, shares = state
    delta = 0.0
    for (start, end), share in zip(spans, shares):
        weight = (exp_buf[start:end] * share).astype(jnp.bfloat16)
        weight_buf[start:end] = weight
        delta = delta + fold(weight.astype(jnp.float32) * slope_buf[start:end], jnp.sum)
    delta = jnp.sum(delta, axis=0, keepdims=True)
    value_terms = dot(weight_buf[...], stack(live, spots, 0))
    for (start, end), share in zip(spans, shares):
        part = exp_buf[start:end] * share * (slope_buf[start:end] - delta)
        prob_buf[start:end] = part.astype(jnp.bfloat16)
    key_terms = dot(prob_buf[...], stack(query_rows, spots, 0)) * SCALE
    own_flip = keys[prefix:].astype(jnp.float32).T.astype(jnp.bfloat16)
    flipped = dot(key_flip[...], prob_buf[:prefix]) + dot(own_flip, prob_buf[prefix:])
    query_grad = (flipped * SCALE).T.astype(jnp.bfloat16)
    for at, (_, slot, _, _) in enumerate(spots):
        span = slice(prefix + at * slots, prefix + (at + 1) * slots)
        dv_sum[slot] += value_terms[span]
        dk_sum[slot] += key_terms[span]
    return key_terms[:prefix], value_terms[:prefix], query_grad


def put_query_grad(dq, spots, query_grad):
    half_rows = query_grad.shape[0] // 2
    for at, (block, slot, half, _) in enumerate(spots):

        def put():
            rows = pl.ds(pl.multiple_of(half * HALF, HALF), HALF)
            for head in range(dq.shape[2] // HD):
                start = at * half_rows + head * HALF
                dq[slot, rows, head * HD : (head + 1) * HD] = query_grad[start : start + HALF]

        if at == 0:
            put()
        else:
            pl.when(block < 2 * dq.shape[0])(put)


def near_kernel(code, chained, plan, query_rows, query_flip, live, live_flip, comp_key, comp_value,
                pair, *refs):
    if chained:
        for done, out in zip(refs[:3], refs[4:7]):
            out[...] = done[...]
        refs = refs[3:]
    (term, dq, dk, dv, dk_sum, dv_sum, key_flip, key_sum, value_sum, listed) = refs[:10]
    bufs = (refs[10:16], refs[16:22])
    count, slots = dq.shape[:2]
    prefix = key_sum.shape[0]
    rows = pair.shape[2]
    prepared = (query_rows, query_flip, live, live_flip)

    def size_of(slot):
        return plan[slot] % 64

    found = 0
    for slot in range(count):
        word = plan[slot]
        listed[found] = 2 * slot
        listed[found + 1] = 2 * slot + 1
        blocks = jnp.where(word % 64 > HALF, 2, 1)
        found = found + jnp.where(word // 64 == code, blocks, 0)
    key_sum[...] = jnp.zeros_like(key_sum)
    value_sum[...] = jnp.zeros_like(value_sum)

    @pl.when(found > 0)
    def _():
        dk_sum[...] = jnp.zeros_like(dk_sum)
        dv_sum[...] = jnp.zeros_like(dv_sum)
        for at in range(pair.shape[0]):
            span = slice(at * rows, (at + 1) * rows)
            for keys, values, *_ in bufs:
                keys[span] = pair[at, 0]
                values[span] = pair[at, 1]
            key_flip[:, span] = pair[at, 0].T

    def spots_at(index):
        one = listed[index]
        other = listed[index + 1]
        valid = index + 1 < found
        slot = jnp.where(valid, other // 2, one // 2)
        return (
            (one, one // 2, one % 2, size_of(one // 2)),
            (jnp.where(valid, other, 2 * count), slot, jnp.where(valid, other % 2, 0),
             jnp.where(valid, size_of(slot), 0)),
        )

    def run(starts):
        all_spots = [spots_at(start) for start in starts]
        states = [
            first_half(spots, prepared, comp_key, comp_value, prefix, buf)
            for spots, buf in zip(all_spots, bufs)
        ]
        done = [
            second_half(state, spots, prepared, key_flip, buf, prefix, dk_sum, dv_sum, dq)
            for state, spots, buf in zip(states, all_spots, bufs)
        ]
        key_sum[...] += sum(each[0] for each in done)
        value_sum[...] += sum(each[1] for each in done)
        for spots, each in zip(all_spots, done):
            put_query_grad(dq, spots, each[2])

    pairs = (found + 1) // 2

    def step(at, carry):
        run((4 * at, 4 * at + 2))
        return carry

    lax.fori_loop(0, pairs // 2, step, 0)

    @pl.when(pairs % 2 == 1)
    def _():
        run((2 * pairs - 2,))

    def finish(index, carry):
        block = listed[index]
        slot = block // 2

        @pl.when(block % 2 == 0)
        def _():
            dk[slot] = dk_sum[slot].astype(jnp.bfloat16)
            dv[slot] = dv_sum[slot].astype(jnp.bfloat16)

            @pl.when(size_of(slot) <= HALF)
            def _():
                dq[slot, HALF:] = jnp.zeros_like(dq[slot, HALF:])

        return carry

    lax.fori_loop(0, found, finish, 0)
    for at in range(pair.shape[0]):
        span = slice(at * rows, (at + 1) * rows)
        term[at, 0] = key_sum[span].astype(term.dtype)
        term[at, 1] = value_sum[span].astype(term.dtype)


def near_grads(code, pair, plan, prepared, comp_key, comp_value, chain, shape, kind):
    count, slots, width = shape
    lanes = 2 * HALF * (width // HD)
    prefix = pair.shape[0] * pair.shape[2]
    extent = prefix + 2 * slots
    vmem = pl.BlockSpec(memory_space=pltpu.VMEM)
    narrow = jax.ShapeDtypeStruct(comp_key.shape, jnp.bfloat16)
    operands = [plan, *prepared, comp_key, comp_value, pair]
    if chain is not None:
        operands += list(chain)
    work = 4
    out = pl.pallas_call(
        functools.partial(near_kernel, code, chain is not None),
        out_shape=[
            jax.ShapeDtypeStruct(pair.shape, kind),
            jax.ShapeDtypeStruct(shape, jnp.bfloat16),
            narrow,
            narrow,
        ],
        in_specs=[pl.BlockSpec(memory_space=pltpu.SMEM)] + [vmem] * (len(operands) - 1),
        out_specs=[vmem] * 4,
        scratch_shapes=[
            pltpu.VMEM(comp_key.shape, jnp.float32),
            pltpu.VMEM(comp_key.shape, jnp.float32),
            pltpu.VMEM((HD, prefix), jnp.bfloat16),
            pltpu.VMEM((prefix, HD), jnp.float32),
            pltpu.VMEM((prefix, HD), jnp.float32),
            pltpu.SMEM((2 * count + 4,), jnp.int32),
        ]
        + 2
        * [
            pltpu.VMEM((extent, HD), jnp.bfloat16),
            pltpu.VMEM((extent, HD), jnp.bfloat16),
            pltpu.VMEM((extent, lanes), jnp.bfloat16),
            pltpu.VMEM((extent, lanes), jnp.float32),
            pltpu.VMEM((extent, lanes), jnp.float32),
            pltpu.VMEM((extent, lanes), jnp.bfloat16),
        ],
        compiler_params=pltpu.CompilerParams(vmem_limit_bytes=24 * 2**20),
        cost_estimate=pl.CostEstimate(
            flops=work * 12 * extent * lanes * HD,
            bytes_accessed=work * 10 * slots * width,
            transcendentals=work * extent * lanes,
        ),
    )(*operands)
    return out[0], out[1:]


SMALL = pltpu.CompilerParams(vmem_limit_bytes=4 * 2**20)


def split_kernel(key, value, pair):
    for head in range(pair.shape[0]):
        columns = slice(head * HD, (head + 1) * HD)
        pair[head, 0] = key[:, columns]
        pair[head, 1] = value[:, columns]


def split_heads(key, value, shards):
    return pl.pallas_call(
        split_kernel,
        out_shape=jax.ShapeDtypeStruct((shards, 2, key.shape[0], HD), key.dtype),
        compiler_params=SMALL,
    )(key, value)


def join_kernel(pair, key, value):
    for head in range(pair.shape[0]):
        columns = slice(head * HD, (head + 1) * HD)
        key[:, columns] = pair[head, 0]
        value[:, columns] = pair[head, 1]


def join_heads(pair):
    shards, _, rows, _ = pair.shape
    whole = jax.ShapeDtypeStruct((rows, shards * HD), pair.dtype)
    return pl.pallas_call(join_kernel, out_shape=[whole, whole], compiler_params=SMALL)(pair)


def shifted(value, steps):
    size, shards = lax.axis_size("dp"), lax.axis_size("mp")
    pairs = []
    for at in range(size):
        for shard in range(shards):
            target = (at + (steps if shard % 2 == 0 else -steps)) % size
            pairs.append((at * shards + shard, target * shards + shard))
    return lax.ppermute(value, ("dp", "mp"), pairs)


def per_device(
    query, comp_key, comp_value, prefix_key, prefix_value, grad_out, owner, group, lengths
):
    axis_count = lax.axis_size("dp")
    shards = lax.axis_size("mp")
    position = lax.axis_index("dp")
    prompt_ids = jnp.arange(owner.shape[0], dtype=jnp.int32)
    holder_of = jnp.sum(jnp.where(group[:, None] == prompt_ids[None, :], owner[None, :], 0), axis=1)
    near = ((holder_of - position + 2 + axis_count) % axis_count).astype(jnp.int32)
    near = jnp.where(lax.axis_index("mp") % 2 == 0, near, 4 - near)

    pair = split_heads(prefix_key[0], prefix_value[0], shards)
    own = lax.all_to_all(pair, "mp", split_axis=0, concat_axis=0, tiled=True)
    low_one = shifted(own, 1)
    up_one = shifted(own, -1)
    plan = near * 64 + lengths
    prepared = prepare(lengths, query, grad_out)
    low_one, prepared = lax.optimization_barrier((low_one, prepared))
    low_two = shifted(low_one, 1)
    up_two = shifted(up_one, -1)
    low_near, _ = lax.optimization_barrier((low_one, up_one))

    def grads(code, pair, chain, kind):
        return near_grads(code, pair, plan, prepared, comp_key, comp_value, chain, query.shape, kind)

    low_term, chain = grads(1, low_near, None, jnp.float32)
    low_two_term, chain = grads(0, low_two, chain, jnp.bfloat16)
    up_two_term, chain = grads(4, up_two, chain, jnp.bfloat16)
    low_back = shifted(low_two_term, -1).astype(jnp.float32)
    up_back = shifted(up_two_term, 1).astype(jnp.float32)
    up_term, chain = grads(3, up_one, chain, jnp.float32)
    low_sum = (low_term + low_back).astype(jnp.bfloat16)
    up_sum = (up_term + up_back).astype(jnp.bfloat16)
    up_sum, chain = lax.optimization_barrier((up_sum, chain))
    low_back = shifted(low_sum, -1).astype(jnp.float32)
    up_back = shifted(up_sum, 1).astype(jnp.float32)
    own_term, chain = grads(2, own, chain, jnp.float32)
    gathered = (own_term + low_back + up_back).astype(jnp.bfloat16)
    back = lax.all_to_all(gathered, "mp", split_axis=0, concat_axis=0, tiled=True)
    key_back, value_back = join_heads(back)
    return chain[0], chain[1], chain[2], key_back[None], value_back[None]


def solution(mesh):
    return jax.shard_map(
        per_device,
        mesh=mesh,
        in_specs=(
            P("dp", None, "mp"),
            P("dp", None, "mp"),
            P("dp", None, "mp"),
            P("dp", "mp", None),
            P("dp", "mp", None),
            P("dp", None, "mp"),
            P(),
            P("dp"),
            P("dp"),
        ),
        out_specs=(
            P("dp", None, "mp"),
            P("dp", None, "mp"),
            P("dp", None, "mp"),
            P("dp", "mp", None),
            P("dp", "mp", None),
        ),
        check_vma=False,
    )
```

```python
import functools

import jax
import jax.numpy as jnp
from jax import lax
from jax.experimental import pallas as pl
from jax.experimental.pallas import tpu as pltpu
from jax.sharding import PartitionSpec as P

HD = 128
SCALE = HD**-0.5
LOG2E = 1.4426950408889634
CHUNK = 128
HALF = 16
HIDDEN = -1e30


def dot(left, right):
    return jnp.dot(left, right, preferred_element_type=jnp.float32)


def fold(value, reduce):
    return reduce(value.reshape(-1, 8, value.shape[-1]), axis=0)


def prepare_kernel(lengths, query, grad_out, query_rows, query_flip, live, live_flip):
    slots = query.shape[1]
    heads = query.shape[2] // HD
    for ref in (query_rows, query_flip, live, live_flip):
        ref[ref.shape[0] - 1] = jnp.zeros_like(ref[0])

    def step(slot, carry):
        for half in range(slots // HALF):
            rows = slice(half * HALF, (half + 1) * HALF)
            cells = [(rows, slice(head * HD, (head + 1) * HD)) for head in range(heads)]
            at = slot * (slots // HALF) + half
            block = jnp.concatenate([query[slot, row, col] for row, col in cells], axis=0)
            query_rows[at] = block
            query_flip[at] = block.T
            row_at = lax.broadcasted_iota(jnp.int32, (HALF, HD), 0) + half * HALF
            block = jnp.concatenate(
                [
                    jnp.where(
                        row_at < lengths[slot], grad_out[slot, row, col].astype(jnp.float32), 0.0
                    ).astype(jnp.bfloat16)
                    for row, col in cells
                ],
                axis=0,
            )
            live[at] = block
            live_flip[at] = block.T
        return carry

    lax.fori_loop(0, query.shape[0], step, 0)


def prepare(lengths, query, grad_out):
    count, slots, width = query.shape
    blocks = count * (slots // HALF) + 1
    rows = HALF * (width // HD)
    vmem = pl.BlockSpec(memory_space=pltpu.VMEM)
    tall = jax.ShapeDtypeStruct((blocks, rows, HD), jnp.bfloat16)
    wide = jax.ShapeDtypeStruct((blocks, HD, rows), jnp.bfloat16)
    return pl.pallas_call(
        prepare_kernel,
        out_shape=[tall, wide, tall, wide],
        in_specs=[pl.BlockSpec(memory_space=pltpu.SMEM), vmem, vmem],
        out_specs=[vmem] * 4,
        compiler_params=pltpu.CompilerParams(vmem_limit_bytes=8 * 2**20),
        cost_estimate=pl.CostEstimate(
            flops=0, bytes_accessed=12 * count * slots * width, transcendentals=0
        ),
    )(lengths, query, grad_out)


def stack(ref, spots, axis):
    return jnp.concatenate([ref[block] for block, _, _, _ in spots], axis=axis)


def first_half(spots, prepared, comp_key, comp_value, prefix, bufs):
    _, query_flip, _, live_flip = prepared
    keys, values, _, slope_buf, exp_buf, _ = bufs
    slots = comp_key.shape[1]
    extent = keys.shape[0]
    for at, (_, slot, _, _) in enumerate(spots):
        keys[prefix + at * slots : prefix + (at + 1) * slots] = comp_key[slot]
        values[prefix + at * slots : prefix + (at + 1) * slots] = comp_value[slot]
    queries = stack(query_flip, spots, 1)
    lanes = queries.shape[1]
    row = lax.broadcasted_iota(jnp.int32, (2 * slots, lanes), 0)
    lane = lax.broadcasted_iota(jnp.int32, (2 * slots, lanes), 1)
    side = lane // (lanes // 2)
    key_at = row % slots
    query_at = lane % HALF + HALF * jnp.where(side == 0, spots[0][2], spots[1][2])
    size = jnp.where(side == 0, spots[0][3], spots[1][3])
    visible = (row // slots == side) & (key_at <= query_at) & (key_at < size)

    spans = [(start, min(start + CHUNK, extent)) for start in range(0, extent, CHUNK)]
    scores = dot(keys[...], queries)
    slope_buf[...] = dot(values[...], stack(live_flip, spots, 1))
    tops, sums = [], []
    for start, end in spans:
        part = scores[start:end]
        if start >= prefix:
            part = jnp.where(visible, part, HIDDEN)
        top = jnp.max(fold(part, jnp.max), axis=0, keepdims=True)
        part = jnp.exp2((part - top) * (SCALE * LOG2E))
        exp_buf[start:end] = part
        tops.append(top)
        sums.append(fold(part, jnp.sum))
    top = functools.reduce(jnp.maximum, tops)
    shares = [jnp.exp2((each - top) * (SCALE * LOG2E)) for each in tops]
    total = sum(part * share for part, share in zip(sums, shares))
    inverse = 1.0 / jnp.sum(total, axis=0, keepdims=True)
    return spans, [share * inverse for share in shares]


def second_half(state, spots, prepared, key_flip, bufs, prefix, dk_sum, dv_sum, dq):
    query_rows, _, live, _ = prepared
    keys, _, weight_buf, slope_buf, exp_buf, prob_buf = bufs
    slots = dk_sum.shape[1]
    spans, shares = state
    delta = 0.0
    for (start, end), share in zip(spans, shares):
        weight = (exp_buf[start:end] * share).astype(jnp.bfloat16)
        weight_buf[start:end] = weight
        delta = delta + fold(weight.astype(jnp.float32) * slope_buf[start:end], jnp.sum)
    delta = jnp.sum(delta, axis=0, keepdims=True)
    value_terms = dot(weight_buf[...], stack(live, spots, 0))
    for (start, end), share in zip(spans, shares):
        part = exp_buf[start:end] * share * (slope_buf[start:end] - delta)
        prob_buf[start:end] = part.astype(jnp.bfloat16)
    key_terms = dot(prob_buf[...], stack(query_rows, spots, 0)) * SCALE
    own_flip = keys[prefix:].astype(jnp.float32).T.astype(jnp.bfloat16)
    flipped = dot(key_flip[...], prob_buf[:prefix]) + dot(own_flip, prob_buf[prefix:])
    query_grad = (flipped * SCALE).T.astype(jnp.bfloat16)
    for at, (_, slot, _, _) in enumerate(spots):
        span = slice(prefix + at * slots, prefix + (at + 1) * slots)
        dv_sum[slot] += value_terms[span]
        dk_sum[slot] += key_terms[span]
    return key_terms[:prefix], value_terms[:prefix], query_grad


def put_query_grad(dq, spots, query_grad):
    half_rows = query_grad.shape[0] // 2
    for at, (block, slot, half, _) in enumerate(spots):

        def put():
            rows = pl.ds(pl.multiple_of(half * HALF, HALF), HALF)
            for head in range(dq.shape[2] // HD):
                start = at * half_rows + head * HALF
                dq[slot, rows, head * HD : (head + 1) * HD] = query_grad[start : start + HALF]

        if at == 0:
            put()
        else:
            pl.when(block < 2 * dq.shape[0])(put)


def near_kernel(code, chained, plan, query_rows, query_flip, live, live_flip, comp_key, comp_value,
                pair, *refs):
    if chained:
        for done, out in zip(refs[:3], refs[4:7]):
            out[...] = done[...]
        refs = refs[3:]
    (term, dq, dk, dv, dk_sum, dv_sum, key_flip, key_sum, value_sum, listed) = refs[:10]
    bufs = (refs[10:16], refs[16:22])
    count, slots = dq.shape[:2]
    prefix = key_sum.shape[0]
    rows = pair.shape[2]
    prepared = (query_rows, query_flip, live, live_flip)

    def size_of(slot):
        return plan[slot] % 64

    found = 0
    for slot in range(count):
        word = plan[slot]
        listed[found] = 2 * slot
        listed[found + 1] = 2 * slot + 1
        blocks = jnp.where(word % 64 > HALF, 2, 1)
        found = found + jnp.where(word // 64 == code, blocks, 0)
    key_sum[...] = jnp.zeros_like(key_sum)
    value_sum[...] = jnp.zeros_like(value_sum)

    @pl.when(found > 0)
    def _():
        dk_sum[...] = jnp.zeros_like(dk_sum)
        dv_sum[...] = jnp.zeros_like(dv_sum)
        for at in range(pair.shape[0]):
            span = slice(at * rows, (at + 1) * rows)
            for keys, values, *_ in bufs:
                keys[span] = pair[at, 0]
                values[span] = pair[at, 1]
            key_flip[:, span] = pair[at, 0].T

    def spots_at(index):
        one = listed[index]
        other = listed[index + 1]
        valid = index + 1 < found
        slot = jnp.where(valid, other // 2, one // 2)
        return (
            (one, one // 2, one % 2, size_of(one // 2)),
            (jnp.where(valid, other, 2 * count), slot, jnp.where(valid, other % 2, 0),
             jnp.where(valid, size_of(slot), 0)),
        )

    def run(starts):
        all_spots = [spots_at(start) for start in starts]
        states = [
            first_half(spots, prepared, comp_key, comp_value, prefix, buf)
            for spots, buf in zip(all_spots, bufs)
        ]
        done = [
            second_half(state, spots, prepared, key_flip, buf, prefix, dk_sum, dv_sum, dq)
            for state, spots, buf in zip(states, all_spots, bufs)
        ]
        key_sum[...] += sum(each[0] for each in done)
        value_sum[...] += sum(each[1] for each in done)
        for spots, each in zip(all_spots, done):
            put_query_grad(dq, spots, each[2])

    pairs = (found + 1) // 2

    def step(at, carry):
        run((4 * at, 4 * at + 2))
        return carry

    lax.fori_loop(0, pairs // 2, step, 0)

    @pl.when(pairs % 2 == 1)
    def _():
        run((2 * pairs - 2,))

    def finish(index, carry):
        block = listed[index]
        slot = block // 2

        @pl.when(block % 2 == 0)
        def _():
            dk[slot] = dk_sum[slot].astype(jnp.bfloat16)
            dv[slot] = dv_sum[slot].astype(jnp.bfloat16)

            @pl.when(size_of(slot) <= HALF)
            def _():
                dq[slot, HALF:] = jnp.zeros_like(dq[slot, HALF:])

        return carry

    lax.fori_loop(0, found, finish, 0)
    for at in range(pair.shape[0]):
        span = slice(at * rows, (at + 1) * rows)
        term[at, 0] = key_sum[span].astype(term.dtype)
        term[at, 1] = value_sum[span].astype(term.dtype)


def near_grads(code, pair, plan, prepared, comp_key, comp_value, chain, shape, kind):
    count, slots, width = shape
    lanes = 2 * HALF * (width // HD)
    prefix = pair.shape[0] * pair.shape[2]
    extent = prefix + 2 * slots
    vmem = pl.BlockSpec(memory_space=pltpu.VMEM)
    narrow = jax.ShapeDtypeStruct(comp_key.shape, jnp.bfloat16)
    operands = [plan, *prepared, comp_key, comp_value, pair]
    if chain is not None:
        operands += list(chain)
    work = 4
    out = pl.pallas_call(
        functools.partial(near_kernel, code, chain is not None),
        out_shape=[
            jax.ShapeDtypeStruct(pair.shape, kind),
            jax.ShapeDtypeStruct(shape, jnp.bfloat16),
            narrow,
            narrow,
        ],
        in_specs=[pl.BlockSpec(memory_space=pltpu.SMEM)] + [vmem] * (len(operands) - 1),
        out_specs=[vmem] * 4,
        scratch_shapes=[
            pltpu.VMEM(comp_key.shape, jnp.float32),
            pltpu.VMEM(comp_key.shape, jnp.float32),
            pltpu.VMEM((HD, prefix), jnp.bfloat16),
            pltpu.VMEM((prefix, HD), jnp.float32),
            pltpu.VMEM((prefix, HD), jnp.float32),
            pltpu.SMEM((2 * count + 4,), jnp.int32),
        ]
        + 2
        * [
            pltpu.VMEM((extent, HD), jnp.bfloat16),
            pltpu.VMEM((extent, HD), jnp.bfloat16),
            pltpu.VMEM((extent, lanes), jnp.bfloat16),
            pltpu.VMEM((extent, lanes), jnp.float32),
            pltpu.VMEM((extent, lanes), jnp.float32),
            pltpu.VMEM((extent, lanes), jnp.bfloat16),
        ],
        compiler_params=pltpu.CompilerParams(vmem_limit_bytes=24 * 2**20),
        cost_estimate=pl.CostEstimate(
            flops=work * 12 * extent * lanes * HD,
            bytes_accessed=work * 10 * slots * width,
            transcendentals=work * extent * lanes,
        ),
    )(*operands)
    return out[0], out[1:]


SMALL = pltpu.CompilerParams(vmem_limit_bytes=4 * 2**20)


def split_kernel(key, value, pair):
    for head in range(pair.shape[0]):
        columns = slice(head * HD, (head + 1) * HD)
        pair[head, 0] = key[:, columns]
        pair[head, 1] = value[:, columns]


def split_heads(key, value, shards):
    return pl.pallas_call(
        split_kernel,
        out_shape=jax.ShapeDtypeStruct((shards, 2, key.shape[0], HD), key.dtype),
        compiler_params=SMALL,
    )(key, value)


def join_kernel(pair, key, value):
    for head in range(pair.shape[0]):
        columns = slice(head * HD, (head + 1) * HD)
        key[:, columns] = pair[head, 0]
        value[:, columns] = pair[head, 1]


def join_heads(pair):
    shards, _, rows, _ = pair.shape
    whole = jax.ShapeDtypeStruct((rows, shards * HD), pair.dtype)
    return pl.pallas_call(join_kernel, out_shape=[whole, whole], compiler_params=SMALL)(pair)


def swapped(value, first):
    size = lax.axis_size("dp")
    return lax.ppermute(
        value, "dp", [(at, (at + (1 if at % 2 == first else -1)) % size) for at in range(size)]
    )


def per_device(
    query, comp_key, comp_value, prefix_key, prefix_value, grad_out, owner, group, lengths
):
    axis_count = lax.axis_size("dp")
    shards = lax.axis_size("mp")
    position = lax.axis_index("dp")
    prompt_ids = jnp.arange(owner.shape[0], dtype=jnp.int32)
    holder_of = jnp.sum(jnp.where(group[:, None] == prompt_ids[None, :], owner[None, :], 0), axis=1)
    near = ((holder_of - position + 2 + axis_count) % axis_count).astype(jnp.int32)
    near = jnp.where(position % 2 == 0, near, 4 - near)

    pair = split_heads(prefix_key[0], prefix_value[0], shards)
    own = lax.all_to_all(pair, "mp", split_axis=0, concat_axis=0, tiled=True)
    even_one = swapped(own, 0)
    odd_one = swapped(own, 1)
    plan = near * 64 + lengths
    prepared = prepare(lengths, query, grad_out)
    even_one, prepared = lax.optimization_barrier((even_one, prepared))
    odd_two = swapped(even_one, 1)
    even_two = swapped(odd_one, 0)

    def grads(code, pair, chain, kind):
        return near_grads(code, pair, plan, prepared, comp_key, comp_value, chain, query.shape, kind)

    odd_two_term, chain = grads(0, odd_two, None, jnp.bfloat16)
    even_two_term, chain = grads(4, even_two, chain, jnp.bfloat16)
    odd_two_term, even_two_term = lax.optimization_barrier((odd_two_term, even_two_term))
    even_back = swapped(odd_two_term, 1).astype(jnp.float32)
    odd_back = swapped(even_two_term, 0).astype(jnp.float32)
    odd_term, chain = grads(1, odd_one, chain, jnp.float32)
    even_term, chain = grads(3, even_one, chain, jnp.float32)
    even_sum = (even_term + even_back).astype(jnp.bfloat16)
    odd_sum = (odd_term + odd_back).astype(jnp.bfloat16)
    odd_sum, even_sum, chain = lax.optimization_barrier((odd_sum, even_sum, chain))
    even_back = swapped(even_sum, 0).astype(jnp.float32)
    odd_back = swapped(odd_sum, 1).astype(jnp.float32)
    own_term, chain = grads(2, own, chain, jnp.float32)
    gathered = (own_term + even_back + odd_back).astype(jnp.bfloat16)
    back = lax.all_to_all(gathered, "mp", split_axis=0, concat_axis=0, tiled=True)
    key_back, value_back = join_heads(back)
    return chain[0], chain[1], chain[2], key_back[None], value_back[None]


def solution(mesh):
    return jax.shard_map(
        per_device,
        mesh=mesh,
        in_specs=(
            P("dp", None, "mp"),
            P("dp", None, "mp"),
            P("dp", None, "mp"),
            P("dp", "mp", None),
            P("dp", "mp", None),
            P("dp", None, "mp"),
            P(),
            P("dp"),
            P("dp"),
        ),
        out_specs=(
            P("dp", None, "mp"),
            P("dp", None, "mp"),
            P("dp", None, "mp"),
            P("dp", "mp", None),
            P("dp", "mp", None),
        ),
        check_vma=False,
    )
```

```python
import functools

import jax
import jax.numpy as jnp
from jax import lax
from jax.experimental import pallas as pl
from jax.experimental.pallas import tpu as pltpu
from jax.sharding import PartitionSpec as P

HD = 128
SCALE = HD**-0.5
LOG2E = 1.4426950408889634
CHUNK = 128
HALF = 16
HIDDEN = -1e30


def dot(left, right):
    return jnp.dot(left, right, preferred_element_type=jnp.float32)


def fold(value, reduce):
    return reduce(value.reshape(-1, 8, value.shape[-1]), axis=0)


def prepare_kernel(lengths, query, grad_out, query_rows, query_flip, live, live_flip):
    slots = query.shape[1]
    heads = query.shape[2] // HD
    for ref in (query_rows, query_flip, live, live_flip):
        ref[ref.shape[0] - 1] = jnp.zeros_like(ref[0])

    def step(slot, carry):
        for half in range(slots // HALF):
            rows = slice(half * HALF, (half + 1) * HALF)
            cells = [(rows, slice(head * HD, (head + 1) * HD)) for head in range(heads)]
            at = slot * (slots // HALF) + half
            block = jnp.concatenate([query[slot, row, col] for row, col in cells], axis=0)
            query_rows[at] = block
            query_flip[at] = block.T
            row_at = lax.broadcasted_iota(jnp.int32, (HALF, HD), 0) + half * HALF
            block = jnp.concatenate(
                [
                    jnp.where(
                        row_at < lengths[slot], grad_out[slot, row, col].astype(jnp.float32), 0.0
                    ).astype(jnp.bfloat16)
                    for row, col in cells
                ],
                axis=0,
            )
            live[at] = block
            live_flip[at] = block.T
        return carry

    lax.fori_loop(0, query.shape[0], step, 0)


def prepare(lengths, query, grad_out):
    count, slots, width = query.shape
    blocks = count * (slots // HALF) + 1
    rows = HALF * (width // HD)
    vmem = pl.BlockSpec(memory_space=pltpu.VMEM)
    tall = jax.ShapeDtypeStruct((blocks, rows, HD), jnp.bfloat16)
    wide = jax.ShapeDtypeStruct((blocks, HD, rows), jnp.bfloat16)
    return pl.pallas_call(
        prepare_kernel,
        out_shape=[tall, wide, tall, wide],
        in_specs=[pl.BlockSpec(memory_space=pltpu.SMEM), vmem, vmem],
        out_specs=[vmem] * 4,
        compiler_params=pltpu.CompilerParams(vmem_limit_bytes=8 * 2**20),
        cost_estimate=pl.CostEstimate(
            flops=0, bytes_accessed=12 * count * slots * width, transcendentals=0
        ),
    )(lengths, query, grad_out)


def stack(ref, spots, axis):
    return jnp.concatenate([ref[block] for block, _, _, _ in spots], axis=axis)


def first_half(spots, prepared, comp_key, comp_value, prefix, bufs):
    _, query_flip, _, live_flip = prepared
    keys, values, _, slope_buf, exp_buf, _ = bufs
    slots = comp_key.shape[1]
    extent = keys.shape[0]
    for at, (_, slot, _, _) in enumerate(spots):
        keys[prefix + at * slots : prefix + (at + 1) * slots] = comp_key[slot]
        values[prefix + at * slots : prefix + (at + 1) * slots] = comp_value[slot]
    queries = stack(query_flip, spots, 1)
    lanes = queries.shape[1]
    row = lax.broadcasted_iota(jnp.int32, (2 * slots, lanes), 0)
    lane = lax.broadcasted_iota(jnp.int32, (2 * slots, lanes), 1)
    side = lane // (lanes // 2)
    key_at = row % slots
    query_at = lane % HALF + HALF * jnp.where(side == 0, spots[0][2], spots[1][2])
    size = jnp.where(side == 0, spots[0][3], spots[1][3])
    visible = (row // slots == side) & (key_at <= query_at) & (key_at < size)

    spans = [(start, min(start + CHUNK, extent)) for start in range(0, extent, CHUNK)]
    scores = dot(keys[...], queries)
    slope_buf[...] = dot(values[...], stack(live_flip, spots, 1))
    tops, sums = [], []
    for start, end in spans:
        part = scores[start:end]
        if start >= prefix:
            part = jnp.where(visible, part, HIDDEN)
        top = jnp.max(fold(part, jnp.max), axis=0, keepdims=True)
        part = jnp.exp2((part - top) * (SCALE * LOG2E))
        exp_buf[start:end] = part
        tops.append(top)
        sums.append(fold(part, jnp.sum))
    top = functools.reduce(jnp.maximum, tops)
    shares = [jnp.exp2((each - top) * (SCALE * LOG2E)) for each in tops]
    total = sum(part * share for part, share in zip(sums, shares))
    inverse = 1.0 / jnp.sum(total, axis=0, keepdims=True)
    return spans, [share * inverse for share in shares]


def second_half(state, spots, prepared, key_flip, bufs, prefix, dk_sum, dv_sum, dq):
    query_rows, _, live, _ = prepared
    keys, _, weight_buf, slope_buf, exp_buf, prob_buf = bufs
    slots = dk_sum.shape[1]
    spans, shares = state
    delta = 0.0
    for (start, end), share in zip(spans, shares):
        weight = (exp_buf[start:end] * share).astype(jnp.bfloat16)
        weight_buf[start:end] = weight
        delta = delta + fold(weight.astype(jnp.float32) * slope_buf[start:end], jnp.sum)
    delta = jnp.sum(delta, axis=0, keepdims=True)
    value_terms = dot(weight_buf[...], stack(live, spots, 0))
    for (start, end), share in zip(spans, shares):
        part = exp_buf[start:end] * share * (slope_buf[start:end] - delta)
        prob_buf[start:end] = part.astype(jnp.bfloat16)
    key_terms = dot(prob_buf[...], stack(query_rows, spots, 0)) * SCALE
    own_flip = keys[prefix:].astype(jnp.float32).T.astype(jnp.bfloat16)
    flipped = dot(key_flip[...], prob_buf[:prefix]) + dot(own_flip, prob_buf[prefix:])
    query_grad = (flipped * SCALE).T.astype(jnp.bfloat16)
    for at, (_, slot, _, _) in enumerate(spots):
        span = slice(prefix + at * slots, prefix + (at + 1) * slots)
        dv_sum[slot] += value_terms[span]
        dk_sum[slot] += key_terms[span]
    return key_terms[:prefix], value_terms[:prefix], query_grad


def put_query_grad(dq, spots, query_grad):
    half_rows = query_grad.shape[0] // 2
    for at, (block, slot, half, _) in enumerate(spots):

        def put():
            rows = pl.ds(pl.multiple_of(half * HALF, HALF), HALF)
            for head in range(dq.shape[2] // HD):
                start = at * half_rows + head * HALF
                dq[slot, rows, head * HD : (head + 1) * HD] = query_grad[start : start + HALF]

        if at == 0:
            put()
        else:
            pl.when(block < 2 * dq.shape[0])(put)


def near_kernel(code, chained, plan, query_rows, query_flip, live, live_flip, comp_key, comp_value,
                near_key, near_value, *refs):
    if chained:
        for done, out in zip(refs[:3], refs[5:8]):
            out[...] = done[...]
        refs = refs[3:]
    (key_term, value_term, dq, dk, dv, dk_sum, dv_sum, key_flip, key_sum, value_sum, listed) = refs[:11]
    bufs = (refs[11:17], refs[17:23])
    count, slots = dq.shape[:2]
    prefix = key_sum.shape[0]
    rows = near_key.shape[1]
    prepared = (query_rows, query_flip, live, live_flip)

    def size_of(slot):
        return plan[slot] % 64

    found = 0
    for slot in range(count):
        word = plan[slot]
        listed[found] = 2 * slot
        listed[found + 1] = 2 * slot + 1
        blocks = jnp.where(word % 64 > HALF, 2, 1)
        found = found + jnp.where(word // 64 == code, blocks, 0)
    key_sum[...] = jnp.zeros_like(key_sum)
    value_sum[...] = jnp.zeros_like(value_sum)

    @pl.when(found > 0)
    def _():
        dk_sum[...] = jnp.zeros_like(dk_sum)
        dv_sum[...] = jnp.zeros_like(dv_sum)
        for at in range(near_key.shape[0]):
            span = slice(at * rows, (at + 1) * rows)
            for keys, values, *_ in bufs:
                keys[span] = near_key[at]
                values[span] = near_value[at]
            key_flip[:, span] = near_key[at].T

    def spots_at(index):
        one = listed[index]
        other = listed[index + 1]
        valid = index + 1 < found
        slot = jnp.where(valid, other // 2, one // 2)
        return (
            (one, one // 2, one % 2, size_of(one // 2)),
            (jnp.where(valid, other, 2 * count), slot, jnp.where(valid, other % 2, 0),
             jnp.where(valid, size_of(slot), 0)),
        )

    def run(starts):
        all_spots = [spots_at(start) for start in starts]
        states = [
            first_half(spots, prepared, comp_key, comp_value, prefix, buf)
            for spots, buf in zip(all_spots, bufs)
        ]
        done = [
            second_half(state, spots, prepared, key_flip, buf, prefix, dk_sum, dv_sum, dq)
            for state, spots, buf in zip(states, all_spots, bufs)
        ]
        key_sum[...] += sum(each[0] for each in done)
        value_sum[...] += sum(each[1] for each in done)
        for spots, each in zip(all_spots, done):
            put_query_grad(dq, spots, each[2])

    pairs = (found + 1) // 2

    def step(at, carry):
        run((4 * at, 4 * at + 2))
        return carry

    lax.fori_loop(0, pairs // 2, step, 0)

    @pl.when(pairs % 2 == 1)
    def _():
        run((2 * pairs - 2,))

    def finish(index, carry):
        block = listed[index]
        slot = block // 2

        @pl.when(block % 2 == 0)
        def _():
            dk[slot] = dk_sum[slot].astype(jnp.bfloat16)
            dv[slot] = dv_sum[slot].astype(jnp.bfloat16)

            @pl.when(size_of(slot) <= HALF)
            def _():
                dq[slot, HALF:] = jnp.zeros_like(dq[slot, HALF:])

        return carry

    lax.fori_loop(0, found, finish, 0)
    for at in range(near_key.shape[0]):
        span = slice(at * rows, (at + 1) * rows)
        key_term[at] = key_sum[span].astype(key_term.dtype)
        value_term[at] = value_sum[span].astype(value_term.dtype)


def near_grads(code, pair, plan, prepared, comp_key, comp_value, chain, shape, kind):
    count, slots, width = shape
    lanes = 2 * HALF * (width // HD)
    prefix = pair[0].shape[0] * pair[0].shape[1]
    extent = prefix + 2 * slots
    vmem = pl.BlockSpec(memory_space=pltpu.VMEM)
    narrow = jax.ShapeDtypeStruct(comp_key.shape, jnp.bfloat16)
    operands = [plan, *prepared, comp_key, comp_value, *pair]
    if chain is not None:
        operands += list(chain)
    work = 4
    out = pl.pallas_call(
        functools.partial(near_kernel, code, chain is not None),
        out_shape=[
            jax.ShapeDtypeStruct(pair[0].shape, kind),
            jax.ShapeDtypeStruct(pair[0].shape, kind),
            jax.ShapeDtypeStruct(shape, jnp.bfloat16),
            narrow,
            narrow,
        ],
        in_specs=[pl.BlockSpec(memory_space=pltpu.SMEM)] + [vmem] * (len(operands) - 1),
        out_specs=[vmem] * 5,
        scratch_shapes=[
            pltpu.VMEM(comp_key.shape, jnp.float32),
            pltpu.VMEM(comp_key.shape, jnp.float32),
            pltpu.VMEM((HD, prefix), jnp.bfloat16),
            pltpu.VMEM((prefix, HD), jnp.float32),
            pltpu.VMEM((prefix, HD), jnp.float32),
            pltpu.SMEM((2 * count + 4,), jnp.int32),
        ]
        + 2
        * [
            pltpu.VMEM((extent, HD), jnp.bfloat16),
            pltpu.VMEM((extent, HD), jnp.bfloat16),
            pltpu.VMEM((extent, lanes), jnp.bfloat16),
            pltpu.VMEM((extent, lanes), jnp.float32),
            pltpu.VMEM((extent, lanes), jnp.float32),
            pltpu.VMEM((extent, lanes), jnp.bfloat16),
        ],
        compiler_params=pltpu.CompilerParams(vmem_limit_bytes=24 * 2**20),
        cost_estimate=pl.CostEstimate(
            flops=work * 12 * extent * lanes * HD,
            bytes_accessed=work * 10 * slots * width,
            transcendentals=work * extent * lanes,
        ),
    )(*operands)
    return out[:2], out[2:]


SMALL = pltpu.CompilerParams(vmem_limit_bytes=4 * 2**20)


def split_kernel(key, value, pair):
    for head in range(pair.shape[0]):
        columns = slice(head * HD, (head + 1) * HD)
        pair[head, 0] = key[:, columns]
        pair[head, 1] = value[:, columns]


def split_heads(key, value, shards):
    return pl.pallas_call(
        split_kernel,
        out_shape=jax.ShapeDtypeStruct((shards, 2, key.shape[0], HD), key.dtype),
        compiler_params=SMALL,
    )(key, value)


def part_kernel(pair, key, value):
    key[...] = pair[:, 0]
    value[...] = pair[:, 1]


def parted(pair):
    shards, _, rows, _ = pair.shape
    half = jax.ShapeDtypeStruct((shards, rows, HD), pair.dtype)
    return pl.pallas_call(part_kernel, out_shape=[half, half], compiler_params=SMALL)(pair)


def join_kernel(key_parts, value_parts, key, value):
    for head in range(key_parts.shape[0]):
        columns = slice(head * HD, (head + 1) * HD)
        key[:, columns] = key_parts[head]
        value[:, columns] = value_parts[head]


def join_heads(key_parts, value_parts):
    shards, rows, _ = key_parts.shape
    whole = jax.ShapeDtypeStruct((rows, shards * HD), key_parts.dtype)
    return pl.pallas_call(join_kernel, out_shape=[whole, whole], compiler_params=SMALL)(
        key_parts, value_parts
    )


def wide(terms):
    return [term.astype(jnp.float32) for term in terms]


def added(*terms):
    return [sum(parts).astype(jnp.bfloat16) for parts in zip(*terms)]


def swapped(value, first):
    size = lax.axis_size("dp")
    return lax.ppermute(
        value, "dp", [(at, (at + (1 if at % 2 == first else -1)) % size) for at in range(size)]
    )


def exchanged(for_even, for_odd):
    parts = [(swapped(one, 0), swapped(other, 1)) for one, other in zip(for_even, for_odd)]
    return [one for one, _ in parts], [other for _, other in parts]


def per_device(
    query, comp_key, comp_value, prefix_key, prefix_value, grad_out, owner, group, lengths
):
    axis_count = lax.axis_size("dp")
    shards = lax.axis_size("mp")
    position = lax.axis_index("dp")
    prompt_ids = jnp.arange(owner.shape[0], dtype=jnp.int32)
    holder_of = jnp.sum(jnp.where(group[:, None] == prompt_ids[None, :], owner[None, :], 0), axis=1)
    near = ((holder_of - position + 2 + axis_count) % axis_count).astype(jnp.int32)
    near = jnp.where(position % 2 == 0, near, 4 - near)

    pair = split_heads(prefix_key[0], prefix_value[0], shards)
    own = parted(lax.all_to_all(pair, "mp", split_axis=0, concat_axis=0, tiled=True))
    even_one, odd_one = exchanged(own, own)
    plan = near * 64 + lengths
    prepared = prepare(lengths, query, grad_out)
    even_one[0], prepared = lax.optimization_barrier((even_one[0], prepared))
    even_two, odd_two = exchanged(odd_one, even_one)

    def grads(code, pair, chain, kind):
        return near_grads(code, pair, plan, prepared, comp_key, comp_value, chain, query.shape, kind)

    odd_two_term, chain = grads(0, odd_two, None, jnp.bfloat16)
    even_two_term, chain = grads(4, even_two, chain, jnp.bfloat16)
    odd_two_term, even_two_term = lax.optimization_barrier((odd_two_term, even_two_term))
    odd_back, even_back = exchanged(even_two_term, odd_two_term)
    odd_term, chain = grads(1, odd_one, chain, jnp.float32)
    even_term, chain = grads(3, even_one, chain, jnp.float32)
    even_sum = added(even_term, wide(even_back))
    odd_sum = added(odd_term, wide(odd_back))
    even_back, odd_back = exchanged(even_sum, odd_sum)
    odd_sum, even_sum, chain = lax.optimization_barrier((odd_sum, even_sum, chain))
    own_term, chain = grads(2, own, chain, jnp.float32)
    gathered = added(own_term, wide(even_back), wide(odd_back))
    key_back, value_back = join_heads(
        *(lax.all_to_all(part, "mp", split_axis=0, concat_axis=0, tiled=True) for part in gathered)
    )
    return chain[0], chain[1], chain[2], key_back[None], value_back[None]


def solution(mesh):
    return jax.shard_map(
        per_device,
        mesh=mesh,
        in_specs=(
            P("dp", None, "mp"),
            P("dp", None, "mp"),
            P("dp", None, "mp"),
            P("dp", "mp", None),
            P("dp", "mp", None),
            P("dp", None, "mp"),
            P(),
            P("dp"),
            P("dp"),
        ),
        out_specs=(
            P("dp", None, "mp"),
            P("dp", None, "mp"),
            P("dp", None, "mp"),
            P("dp", "mp", None),
            P("dp", "mp", None),
        ),
        check_vma=False,
    )
```

```python
import functools

import jax
import jax.numpy as jnp
from jax import lax
from jax.experimental import pallas as pl
from jax.experimental.pallas import tpu as pltpu
from jax.sharding import PartitionSpec as P

HD = 128
SCALE = HD**-0.5
LOG2E = 1.4426950408889634
CHUNK = 128
HALF = 16
HIDDEN = -1e30


def dot(left, right):
    return jnp.dot(left, right, preferred_element_type=jnp.float32)


def fold(value, reduce):
    return reduce(value.reshape(-1, 8, value.shape[-1]), axis=0)


def prepare_kernel(lengths, query, grad_out, query_rows, query_flip, live, live_flip):
    slots = query.shape[1]
    heads = query.shape[2] // HD
    for ref in (query_rows, query_flip, live, live_flip):
        ref[ref.shape[0] - 1] = jnp.zeros_like(ref[0])

    def step(slot, carry):
        for half in range(slots // HALF):
            rows = slice(half * HALF, (half + 1) * HALF)
            cells = [(rows, slice(head * HD, (head + 1) * HD)) for head in range(heads)]
            at = slot * (slots // HALF) + half
            block = jnp.concatenate([query[slot, row, col] for row, col in cells], axis=0)
            query_rows[at] = block
            query_flip[at] = block.T
            row_at = lax.broadcasted_iota(jnp.int32, (HALF, HD), 0) + half * HALF
            block = jnp.concatenate(
                [
                    jnp.where(
                        row_at < lengths[slot], grad_out[slot, row, col].astype(jnp.float32), 0.0
                    ).astype(jnp.bfloat16)
                    for row, col in cells
                ],
                axis=0,
            )
            live[at] = block
            live_flip[at] = block.T
        return carry

    lax.fori_loop(0, query.shape[0], step, 0)


def prepare(lengths, query, grad_out):
    count, slots, width = query.shape
    blocks = count * (slots // HALF) + 1
    rows = HALF * (width // HD)
    vmem = pl.BlockSpec(memory_space=pltpu.VMEM)
    tall = jax.ShapeDtypeStruct((blocks, rows, HD), jnp.bfloat16)
    wide = jax.ShapeDtypeStruct((blocks, HD, rows), jnp.bfloat16)
    return pl.pallas_call(
        prepare_kernel,
        out_shape=[tall, wide, tall, wide],
        in_specs=[pl.BlockSpec(memory_space=pltpu.SMEM), vmem, vmem],
        out_specs=[vmem] * 4,
        compiler_params=pltpu.CompilerParams(vmem_limit_bytes=8 * 2**20),
        cost_estimate=pl.CostEstimate(
            flops=0, bytes_accessed=12 * count * slots * width, transcendentals=0
        ),
    )(lengths, query, grad_out)


def stack(ref, spots, axis):
    return jnp.concatenate([ref[block] for block, _, _, _ in spots], axis=axis)


def first_half(spots, prepared, comp_key, comp_value, prefix, bufs):
    _, query_flip, _, live_flip = prepared
    keys, values, _, slope_buf, exp_buf, _ = bufs
    slots = comp_key.shape[1]
    extent = keys.shape[0]
    for at, (_, slot, _, _) in enumerate(spots):
        keys[prefix + at * slots : prefix + (at + 1) * slots] = comp_key[slot]
        values[prefix + at * slots : prefix + (at + 1) * slots] = comp_value[slot]
    queries = stack(query_flip, spots, 1)
    lanes = queries.shape[1]
    row = lax.broadcasted_iota(jnp.int32, (2 * slots, lanes), 0)
    lane = lax.broadcasted_iota(jnp.int32, (2 * slots, lanes), 1)
    side = lane // (lanes // 2)
    key_at = row % slots
    query_at = lane % HALF + HALF * jnp.where(side == 0, spots[0][2], spots[1][2])
    size = jnp.where(side == 0, spots[0][3], spots[1][3])
    visible = (row // slots == side) & (key_at <= query_at) & (key_at < size)

    spans = [(start, min(start + CHUNK, extent)) for start in range(0, extent, CHUNK)]
    scores = dot(keys[...], queries)
    slope_buf[...] = dot(values[...], stack(live_flip, spots, 1))
    tops, sums = [], []
    for start, end in spans:
        part = scores[start:end]
        if start >= prefix:
            part = jnp.where(visible, part, HIDDEN)
        top = jnp.max(fold(part, jnp.max), axis=0, keepdims=True)
        part = jnp.exp2((part - top) * (SCALE * LOG2E))
        exp_buf[start:end] = part
        tops.append(top)
        sums.append(fold(part, jnp.sum))
    top = functools.reduce(jnp.maximum, tops)
    shares = [jnp.exp2((each - top) * (SCALE * LOG2E)) for each in tops]
    total = sum(part * share for part, share in zip(sums, shares))
    inverse = 1.0 / jnp.sum(total, axis=0, keepdims=True)
    return spans, [share * inverse for share in shares]


def second_half(state, spots, prepared, key_flip, bufs, prefix, dk_sum, dv_sum, dq):
    query_rows, _, live, _ = prepared
    keys, _, weight_buf, slope_buf, exp_buf, prob_buf = bufs
    slots = dk_sum.shape[1]
    spans, shares = state
    delta = 0.0
    for (start, end), share in zip(spans, shares):
        weight = (exp_buf[start:end] * share).astype(jnp.bfloat16)
        weight_buf[start:end] = weight
        delta = delta + fold(weight.astype(jnp.float32) * slope_buf[start:end], jnp.sum)
    delta = jnp.sum(delta, axis=0, keepdims=True)
    value_terms = dot(weight_buf[...], stack(live, spots, 0))
    for (start, end), share in zip(spans, shares):
        part = exp_buf[start:end] * share * (slope_buf[start:end] - delta)
        prob_buf[start:end] = part.astype(jnp.bfloat16)
    key_terms = dot(prob_buf[...], stack(query_rows, spots, 0)) * SCALE
    own_flip = keys[prefix:].astype(jnp.float32).T.astype(jnp.bfloat16)
    flipped = dot(key_flip[...], prob_buf[:prefix]) + dot(own_flip, prob_buf[prefix:])
    query_grad = (flipped * SCALE).T.astype(jnp.bfloat16)
    for at, (_, slot, _, _) in enumerate(spots):
        span = slice(prefix + at * slots, prefix + (at + 1) * slots)
        dv_sum[slot] += value_terms[span]
        dk_sum[slot] += key_terms[span]
    return key_terms[:prefix], value_terms[:prefix], query_grad


def put_query_grad(dq, spots, query_grad):
    half_rows = query_grad.shape[0] // 2
    for at, (block, slot, half, _) in enumerate(spots):

        def put():
            rows = pl.ds(pl.multiple_of(half * HALF, HALF), HALF)
            for head in range(dq.shape[2] // HD):
                start = at * half_rows + head * HALF
                dq[slot, rows, head * HD : (head + 1) * HD] = query_grad[start : start + HALF]

        if at == 0:
            put()
        else:
            pl.when(block < 2 * dq.shape[0])(put)


def near_kernel(code, chained, plan, query_rows, query_flip, live, live_flip, comp_key, comp_value,
                pair, *refs):
    if chained:
        for done, out in zip(refs[:3], refs[4:7]):
            out[...] = done[...]
        refs = refs[3:]
    (term, dq, dk, dv, dk_sum, dv_sum, key_flip, key_sum, value_sum, listed) = refs[:10]
    bufs = (refs[10:16], refs[16:22])
    count, slots = dq.shape[:2]
    prefix = key_sum.shape[0]
    rows = pair.shape[2]
    prepared = (query_rows, query_flip, live, live_flip)

    def size_of(slot):
        return plan[slot] % 64

    found = 0
    for slot in range(count):
        word = plan[slot]
        listed[found] = 2 * slot
        listed[found + 1] = 2 * slot + 1
        blocks = jnp.where(word % 64 > HALF, 2, 1)
        found = found + jnp.where(word // 64 == code, blocks, 0)
    key_sum[...] = jnp.zeros_like(key_sum)
    value_sum[...] = jnp.zeros_like(value_sum)

    @pl.when(found > 0)
    def _():
        dk_sum[...] = jnp.zeros_like(dk_sum)
        dv_sum[...] = jnp.zeros_like(dv_sum)
        for at in range(pair.shape[0]):
            span = slice(at * rows, (at + 1) * rows)
            for keys, values, *_ in bufs:
                keys[span] = pair[at, 0]
                values[span] = pair[at, 1]
            key_flip[:, span] = pair[at, 0].T

    def spots_at(index):
        one = listed[index]
        other = listed[index + 1]
        valid = index + 1 < found
        slot = jnp.where(valid, other // 2, one // 2)
        return (
            (one, one // 2, one % 2, size_of(one // 2)),
            (jnp.where(valid, other, 2 * count), slot, jnp.where(valid, other % 2, 0),
             jnp.where(valid, size_of(slot), 0)),
        )

    def run(starts):
        all_spots = [spots_at(start) for start in starts]
        states = [
            first_half(spots, prepared, comp_key, comp_value, prefix, buf)
            for spots, buf in zip(all_spots, bufs)
        ]
        done = [
            second_half(state, spots, prepared, key_flip, buf, prefix, dk_sum, dv_sum, dq)
            for state, spots, buf in zip(states, all_spots, bufs)
        ]
        key_sum[...] += sum(each[0] for each in done)
        value_sum[...] += sum(each[1] for each in done)
        for spots, each in zip(all_spots, done):
            put_query_grad(dq, spots, each[2])

    pairs = (found + 1) // 2

    def step(at, carry):
        run((4 * at, 4 * at + 2))
        return carry

    lax.fori_loop(0, pairs // 2, step, 0)

    @pl.when(pairs % 2 == 1)
    def _():
        run((2 * pairs - 2,))

    def finish(index, carry):
        block = listed[index]
        slot = block // 2

        @pl.when(block % 2 == 0)
        def _():
            dk[slot] = dk_sum[slot].astype(jnp.bfloat16)
            dv[slot] = dv_sum[slot].astype(jnp.bfloat16)

            @pl.when(size_of(slot) <= HALF)
            def _():
                dq[slot, HALF:] = jnp.zeros_like(dq[slot, HALF:])

        return carry

    lax.fori_loop(0, found, finish, 0)
    for at in range(pair.shape[0]):
        span = slice(at * rows, (at + 1) * rows)
        term[at, 0] = key_sum[span].astype(term.dtype)
        term[at, 1] = value_sum[span].astype(term.dtype)


def near_grads(code, pair, plan, prepared, comp_key, comp_value, chain, shape, kind):
    count, slots, width = shape
    lanes = 2 * HALF * (width // HD)
    prefix = pair.shape[0] * pair.shape[2]
    extent = prefix + 2 * slots
    vmem = pl.BlockSpec(memory_space=pltpu.VMEM)
    narrow = jax.ShapeDtypeStruct(comp_key.shape, jnp.bfloat16)
    operands = [plan, *prepared, comp_key, comp_value, pair]
    if chain is not None:
        operands += list(chain)
    work = 4
    out = pl.pallas_call(
        functools.partial(near_kernel, code, chain is not None),
        out_shape=[
            jax.ShapeDtypeStruct(pair.shape, kind),
            jax.ShapeDtypeStruct(shape, jnp.bfloat16),
            narrow,
            narrow,
        ],
        in_specs=[pl.BlockSpec(memory_space=pltpu.SMEM)] + [vmem] * (len(operands) - 1),
        out_specs=[vmem] * 4,
        scratch_shapes=[
            pltpu.VMEM(comp_key.shape, jnp.float32),
            pltpu.VMEM(comp_key.shape, jnp.float32),
            pltpu.VMEM((HD, prefix), jnp.bfloat16),
            pltpu.VMEM((prefix, HD), jnp.float32),
            pltpu.VMEM((prefix, HD), jnp.float32),
            pltpu.SMEM((2 * count + 4,), jnp.int32),
        ]
        + 2
        * [
            pltpu.VMEM((extent, HD), jnp.bfloat16),
            pltpu.VMEM((extent, HD), jnp.bfloat16),
            pltpu.VMEM((extent, lanes), jnp.bfloat16),
            pltpu.VMEM((extent, lanes), jnp.float32),
            pltpu.VMEM((extent, lanes), jnp.float32),
            pltpu.VMEM((extent, lanes), jnp.bfloat16),
        ],
        compiler_params=pltpu.CompilerParams(vmem_limit_bytes=24 * 2**20),
        cost_estimate=pl.CostEstimate(
            flops=work * 12 * extent * lanes * HD,
            bytes_accessed=work * 10 * slots * width,
            transcendentals=work * extent * lanes,
        ),
    )(*operands)
    return out[0], out[1:]


SMALL = pltpu.CompilerParams(vmem_limit_bytes=4 * 2**20)


def split_kernel(key, value, pair):
    for head in range(pair.shape[0]):
        columns = slice(head * HD, (head + 1) * HD)
        pair[head, 0] = key[:, columns]
        pair[head, 1] = value[:, columns]


def split_heads(key, value, shards):
    return pl.pallas_call(
        split_kernel,
        out_shape=jax.ShapeDtypeStruct((shards, 2, key.shape[0], HD), key.dtype),
        compiler_params=SMALL,
    )(key, value)


def join_kernel(pair, key, value):
    for head in range(pair.shape[0]):
        columns = slice(head * HD, (head + 1) * HD)
        key[:, columns] = pair[head, 0]
        value[:, columns] = pair[head, 1]


def join_heads(pair):
    shards, _, rows, _ = pair.shape
    whole = jax.ShapeDtypeStruct((rows, shards * HD), pair.dtype)
    return pl.pallas_call(join_kernel, out_shape=[whole, whole], compiler_params=SMALL)(pair)


def shifted(value, steps):
    size, shards = lax.axis_size("dp"), lax.axis_size("mp")
    pairs = []
    for at in range(size):
        for shard in range(shards):
            target = (at + (steps if shard % 2 == 0 else -steps)) % size
            pairs.append((at * shards + shard, target * shards + shard))
    return lax.ppermute(value, ("dp", "mp"), pairs)


def per_device(
    query, comp_key, comp_value, prefix_key, prefix_value, grad_out, owner, group, lengths
):
    axis_count = lax.axis_size("dp")
    shards = lax.axis_size("mp")
    position = lax.axis_index("dp")
    prompt_ids = jnp.arange(owner.shape[0], dtype=jnp.int32)
    holder_of = jnp.sum(jnp.where(group[:, None] == prompt_ids[None, :], owner[None, :], 0), axis=1)
    near = ((holder_of - position + 2 + axis_count) % axis_count).astype(jnp.int32)
    near = jnp.where(lax.axis_index("mp") % 2 == 0, near, 4 - near)

    pair = split_heads(prefix_key[0], prefix_value[0], shards)
    own = lax.all_to_all(pair, "mp", split_axis=0, concat_axis=0, tiled=True)
    low_one = shifted(own, 1)
    up_one = shifted(own, -1)
    plan = near * 64 + lengths
    prepared = prepare(lengths, query, grad_out)
    low_one, prepared = lax.optimization_barrier((low_one, prepared))
    low_two = shifted(low_one, 1)
    up_two = shifted(up_one, -1)

    def grads(code, pair, chain, kind):
        return near_grads(code, pair, plan, prepared, comp_key, comp_value, chain, query.shape, kind)

    low_two_term, chain = grads(0, low_two, None, jnp.bfloat16)
    up_two_term, chain = grads(4, up_two, chain, jnp.bfloat16)
    low_two_term, up_two_term = lax.optimization_barrier((low_two_term, up_two_term))
    low_back = shifted(low_two_term, -1).astype(jnp.float32)
    up_back = shifted(up_two_term, 1).astype(jnp.float32)
    low_term, chain = grads(1, low_one, chain, jnp.float32)
    up_term, chain = grads(3, up_one, chain, jnp.float32)
    low_sum = (low_term + low_back).astype(jnp.bfloat16)
    up_sum = (up_term + up_back).astype(jnp.bfloat16)
    low_back = shifted(low_sum, -1).astype(jnp.float32)
    up_back = shifted(up_sum, 1).astype(jnp.float32)
    _, _, chain = lax.optimization_barrier((low_sum, up_sum, chain))
    own_term, chain = grads(2, own, chain, jnp.float32)
    gathered = (own_term + low_back + up_back).astype(jnp.bfloat16)
    back = lax.all_to_all(gathered, "mp", split_axis=0, concat_axis=0, tiled=True)
    key_back, value_back = join_heads(back)
    return chain[0], chain[1], chain[2], key_back[None], value_back[None]


def solution(mesh):
    return jax.shard_map(
        per_device,
        mesh=mesh,
        in_specs=(
            P("dp", None, "mp"),
            P("dp", None, "mp"),
            P("dp", None, "mp"),
            P("dp", "mp", None),
            P("dp", "mp", None),
            P("dp", None, "mp"),
            P(),
            P("dp"),
            P("dp"),
        ),
        out_specs=(
            P("dp", None, "mp"),
            P("dp", None, "mp"),
            P("dp", None, "mp"),
            P("dp", "mp", None),
            P("dp", "mp", None),
        ),
        check_vma=False,
    )
```

```python
import functools

import jax
import jax.numpy as jnp
from jax import lax
from jax.experimental import pallas as pl
from jax.experimental.pallas import tpu as pltpu
from jax.sharding import PartitionSpec as P

HD = 128
SCALE = HD**-0.5
LOG2E = 1.4426950408889634
CHUNK = 128
HALF = 16
HIDDEN = -1e30


def dot(left, right):
    return jnp.dot(left, right, preferred_element_type=jnp.float32)


def fold(value, reduce):
    return reduce(value.reshape(-1, 8, value.shape[-1]), axis=0)


def prepare_kernel(lengths, query, grad_out, query_rows, query_flip, live, live_flip):
    slots = query.shape[1]
    heads = query.shape[2] // HD
    for ref in (query_rows, query_flip, live, live_flip):
        ref[ref.shape[0] - 1] = jnp.zeros_like(ref[0])

    def step(slot, carry):
        for half in range(slots // HALF):
            rows = slice(half * HALF, (half + 1) * HALF)
            cells = [(rows, slice(head * HD, (head + 1) * HD)) for head in range(heads)]
            at = slot * (slots // HALF) + half
            block = jnp.concatenate([query[slot, row, col] for row, col in cells], axis=0)
            query_rows[at] = block
            query_flip[at] = block.T
            row_at = lax.broadcasted_iota(jnp.int32, (HALF, HD), 0) + half * HALF
            block = jnp.concatenate(
                [
                    jnp.where(
                        row_at < lengths[slot], grad_out[slot, row, col].astype(jnp.float32), 0.0
                    ).astype(jnp.bfloat16)
                    for row, col in cells
                ],
                axis=0,
            )
            live[at] = block
            live_flip[at] = block.T
        return carry

    lax.fori_loop(0, query.shape[0], step, 0)


def prepare(lengths, query, grad_out):
    count, slots, width = query.shape
    blocks = count * (slots // HALF) + 1
    rows = HALF * (width // HD)
    vmem = pl.BlockSpec(memory_space=pltpu.VMEM)
    tall = jax.ShapeDtypeStruct((blocks, rows, HD), jnp.bfloat16)
    wide = jax.ShapeDtypeStruct((blocks, HD, rows), jnp.bfloat16)
    return pl.pallas_call(
        prepare_kernel,
        out_shape=[tall, wide, tall, wide],
        in_specs=[pl.BlockSpec(memory_space=pltpu.SMEM), vmem, vmem],
        out_specs=[vmem] * 4,
        compiler_params=pltpu.CompilerParams(vmem_limit_bytes=8 * 2**20),
        cost_estimate=pl.CostEstimate(
            flops=0, bytes_accessed=12 * count * slots * width, transcendentals=0
        ),
    )(lengths, query, grad_out)


def stack(ref, spots, axis):
    return jnp.concatenate([ref[block] for block, _, _, _ in spots], axis=axis)


def first_half(spots, prepared, comp_key, comp_value, prefix, bufs):
    _, query_flip, _, live_flip = prepared
    keys, values, _, slope_buf, exp_buf, _ = bufs
    slots = comp_key.shape[1]
    extent = keys.shape[0]
    for at, (_, slot, _, _) in enumerate(spots):
        keys[prefix + at * slots : prefix + (at + 1) * slots] = comp_key[slot]
        values[prefix + at * slots : prefix + (at + 1) * slots] = comp_value[slot]
    queries = stack(query_flip, spots, 1)
    lanes = queries.shape[1]
    row = lax.broadcasted_iota(jnp.int32, (2 * slots, lanes), 0)
    lane = lax.broadcasted_iota(jnp.int32, (2 * slots, lanes), 1)
    side = lane // (lanes // 2)
    key_at = row % slots
    query_at = lane % HALF + HALF * jnp.where(side == 0, spots[0][2], spots[1][2])
    size = jnp.where(side == 0, spots[0][3], spots[1][3])
    visible = (row // slots == side) & (key_at <= query_at) & (key_at < size)

    spans = [(start, min(start + CHUNK, extent)) for start in range(0, extent, CHUNK)]
    scores = dot(keys[...], queries)
    slope_buf[...] = dot(values[...], stack(live_flip, spots, 1))
    tops, sums = [], []
    for start, end in spans:
        part = scores[start:end]
        if start >= prefix:
            part = jnp.where(visible, part, HIDDEN)
        top = jnp.max(fold(part, jnp.max), axis=0, keepdims=True)
        part = jnp.exp2((part - top) * (SCALE * LOG2E))
        exp_buf[start:end] = part
        tops.append(top)
        sums.append(fold(part, jnp.sum))
    top = functools.reduce(jnp.maximum, tops)
    shares = [jnp.exp2((each - top) * (SCALE * LOG2E)) for each in tops]
    total = sum(part * share for part, share in zip(sums, shares))
    inverse = 1.0 / jnp.sum(total, axis=0, keepdims=True)
    return spans, [share * inverse for share in shares]


def second_half(state, spots, prepared, key_flip, bufs, prefix, dk_sum, dv_sum, dq):
    query_rows, _, live, _ = prepared
    keys, _, weight_buf, slope_buf, exp_buf, prob_buf = bufs
    slots = dk_sum.shape[1]
    spans, shares = state
    delta = 0.0
    for (start, end), share in zip(spans, shares):
        weight = (exp_buf[start:end] * share).astype(jnp.bfloat16)
        weight_buf[start:end] = weight
        delta = delta + fold(weight.astype(jnp.float32) * slope_buf[start:end], jnp.sum)
    delta = jnp.sum(delta, axis=0, keepdims=True)
    value_terms = dot(weight_buf[...], stack(live, spots, 0))
    for (start, end), share in zip(spans, shares):
        part = exp_buf[start:end] * share * (slope_buf[start:end] - delta)
        prob_buf[start:end] = part.astype(jnp.bfloat16)
    key_terms = dot(prob_buf[...], stack(query_rows, spots, 0)) * SCALE
    own_flip = keys[prefix:].astype(jnp.float32).T.astype(jnp.bfloat16)
    flipped = dot(key_flip[...], prob_buf[:prefix]) + dot(own_flip, prob_buf[prefix:])
    query_grad = (flipped * SCALE).T.astype(jnp.bfloat16)
    for at, (_, slot, _, _) in enumerate(spots):
        span = slice(prefix + at * slots, prefix + (at + 1) * slots)
        dv_sum[slot] += value_terms[span]
        dk_sum[slot] += key_terms[span]
    return key_terms[:prefix], value_terms[:prefix], query_grad


def put_query_grad(dq, spots, query_grad):
    half_rows = query_grad.shape[0] // 2
    for at, (block, slot, half, _) in enumerate(spots):

        def put():
            rows = pl.ds(pl.multiple_of(half * HALF, HALF), HALF)
            for head in range(dq.shape[2] // HD):
                start = at * half_rows + head * HALF
                dq[slot, rows, head * HD : (head + 1) * HD] = query_grad[start : start + HALF]

        if at == 0:
            put()
        else:
            pl.when(block < 2 * dq.shape[0])(put)


def near_kernel(code, chained, plan, query_rows, query_flip, live, live_flip, comp_key, comp_value,
                pair, *refs):
    if chained:
        for done, out in zip(refs[:3], refs[4:7]):
            out[...] = done[...]
        refs = refs[3:]
    (term, dq, dk, dv, dk_sum, dv_sum, key_flip, key_sum, value_sum, listed) = refs[:10]
    bufs = (refs[10:16], refs[16:22])
    count, slots = dq.shape[:2]
    prefix = key_sum.shape[0]
    rows = pair.shape[2]
    prepared = (query_rows, query_flip, live, live_flip)

    def size_of(slot):
        return plan[slot] % 64

    found = 0
    for slot in range(count):
        word = plan[slot]
        listed[found] = 2 * slot
        listed[found + 1] = 2 * slot + 1
        blocks = jnp.where(word % 64 > HALF, 2, 1)
        found = found + jnp.where(word // 64 == code, blocks, 0)
    key_sum[...] = jnp.zeros_like(key_sum)
    value_sum[...] = jnp.zeros_like(value_sum)

    @pl.when(found > 0)
    def _():
        dk_sum[...] = jnp.zeros_like(dk_sum)
        dv_sum[...] = jnp.zeros_like(dv_sum)
        for at in range(pair.shape[0]):
            span = slice(at * rows, (at + 1) * rows)
            for keys, values, *_ in bufs:
                keys[span] = pair[at, 0]
                values[span] = pair[at, 1]
            key_flip[:, span] = pair[at, 0].T

    def spots_at(index):
        one = listed[index]
        other = listed[index + 1]
        valid = index + 1 < found
        slot = jnp.where(valid, other // 2, one // 2)
        return (
            (one, one // 2, one % 2, size_of(one // 2)),
            (jnp.where(valid, other, 2 * count), slot, jnp.where(valid, other % 2, 0),
             jnp.where(valid, size_of(slot), 0)),
        )

    def run(starts):
        all_spots = [spots_at(start) for start in starts]
        states = [
            first_half(spots, prepared, comp_key, comp_value, prefix, buf)
            for spots, buf in zip(all_spots, bufs)
        ]
        done = [
            second_half(state, spots, prepared, key_flip, buf, prefix, dk_sum, dv_sum, dq)
            for state, spots, buf in zip(states, all_spots, bufs)
        ]
        key_sum[...] += sum(each[0] for each in done)
        value_sum[...] += sum(each[1] for each in done)
        for spots, each in zip(all_spots, done):
            put_query_grad(dq, spots, each[2])

    pairs = (found + 1) // 2

    def step(at, carry):
        run((4 * at, 4 * at + 2))
        return carry

    lax.fori_loop(0, pairs // 2, step, 0)

    @pl.when(pairs % 2 == 1)
    def _():
        run((2 * pairs - 2,))

    def finish(index, carry):
        block = listed[index]
        slot = block // 2

        @pl.when(block % 2 == 0)
        def _():
            dk[slot] = dk_sum[slot].astype(jnp.bfloat16)
            dv[slot] = dv_sum[slot].astype(jnp.bfloat16)

            @pl.when(size_of(slot) <= HALF)
            def _():
                dq[slot, HALF:] = jnp.zeros_like(dq[slot, HALF:])

        return carry

    lax.fori_loop(0, found, finish, 0)
    for at in range(pair.shape[0]):
        span = slice(at * rows, (at + 1) * rows)
        term[at, 0] = key_sum[span].astype(term.dtype)
        term[at, 1] = value_sum[span].astype(term.dtype)


def near_grads(code, pair, plan, prepared, comp_key, comp_value, chain, shape, kind):
    count, slots, width = shape
    lanes = 2 * HALF * (width // HD)
    prefix = pair.shape[0] * pair.shape[2]
    extent = prefix + 2 * slots
    vmem = pl.BlockSpec(memory_space=pltpu.VMEM)
    narrow = jax.ShapeDtypeStruct(comp_key.shape, jnp.bfloat16)
    operands = [plan, *prepared, comp_key, comp_value, pair]
    if chain is not None:
        operands += list(chain)
    work = 4
    out = pl.pallas_call(
        functools.partial(near_kernel, code, chain is not None),
        out_shape=[
            jax.ShapeDtypeStruct(pair.shape, kind),
            jax.ShapeDtypeStruct(shape, jnp.bfloat16),
            narrow,
            narrow,
        ],
        in_specs=[pl.BlockSpec(memory_space=pltpu.SMEM)] + [vmem] * (len(operands) - 1),
        out_specs=[vmem] * 4,
        scratch_shapes=[
            pltpu.VMEM(comp_key.shape, jnp.float32),
            pltpu.VMEM(comp_key.shape, jnp.float32),
            pltpu.VMEM((HD, prefix), jnp.bfloat16),
            pltpu.VMEM((prefix, HD), jnp.float32),
            pltpu.VMEM((prefix, HD), jnp.float32),
            pltpu.SMEM((2 * count + 4,), jnp.int32),
        ]
        + 2
        * [
            pltpu.VMEM((extent, HD), jnp.bfloat16),
            pltpu.VMEM((extent, HD), jnp.bfloat16),
            pltpu.VMEM((extent, lanes), jnp.bfloat16),
            pltpu.VMEM((extent, lanes), jnp.float32),
            pltpu.VMEM((extent, lanes), jnp.float32),
            pltpu.VMEM((extent, lanes), jnp.bfloat16),
        ],
        compiler_params=pltpu.CompilerParams(vmem_limit_bytes=24 * 2**20),
        cost_estimate=pl.CostEstimate(
            flops=work * 12 * extent * lanes * HD,
            bytes_accessed=work * 10 * slots * width,
            transcendentals=work * extent * lanes,
        ),
    )(*operands)
    return out[0], out[1:]


SMALL = pltpu.CompilerParams(vmem_limit_bytes=4 * 2**20)


def split_kernel(key, value, pair):
    for head in range(pair.shape[0]):
        columns = slice(head * HD, (head + 1) * HD)
        pair[head, 0] = key[:, columns]
        pair[head, 1] = value[:, columns]


def split_heads(key, value, shards):
    return pl.pallas_call(
        split_kernel,
        out_shape=jax.ShapeDtypeStruct((shards, 2, key.shape[0], HD), key.dtype),
        compiler_params=SMALL,
    )(key, value)


def join_kernel(pair, key, value):
    for head in range(pair.shape[0]):
        columns = slice(head * HD, (head + 1) * HD)
        key[:, columns] = pair[head, 0]
        value[:, columns] = pair[head, 1]


def join_heads(pair):
    shards, _, rows, _ = pair.shape
    whole = jax.ShapeDtypeStruct((rows, shards * HD), pair.dtype)
    return pl.pallas_call(join_kernel, out_shape=[whole, whole], compiler_params=SMALL)(pair)


def shifted(value, steps):
    size, shards = lax.axis_size("dp"), lax.axis_size("mp")
    pairs = []
    for at in range(size):
        for shard in range(shards):
            target = (at + (steps if shard % 2 == 0 else -steps)) % size
            pairs.append((at * shards + shard, target * shards + shard))
    return lax.ppermute(value, ("dp", "mp"), pairs)


def per_device(
    query, comp_key, comp_value, prefix_key, prefix_value, grad_out, owner, group, lengths
):
    axis_count = lax.axis_size("dp")
    shards = lax.axis_size("mp")
    position = lax.axis_index("dp")
    prompt_ids = jnp.arange(owner.shape[0], dtype=jnp.int32)
    holder_of = jnp.sum(jnp.where(group[:, None] == prompt_ids[None, :], owner[None, :], 0), axis=1)
    near = ((holder_of - position + 2 + axis_count) % axis_count).astype(jnp.int32)
    near = jnp.where(lax.axis_index("mp") % 2 == 0, near, 4 - near)

    pair = split_heads(prefix_key[0], prefix_value[0], shards)
    own = lax.all_to_all(pair, "mp", split_axis=0, concat_axis=0, tiled=True)
    low_one = shifted(own, 1)
    up_one = shifted(own, -1)
    plan = near * 64 + lengths
    prepared = prepare(lengths, query, grad_out)
    low_one, prepared = lax.optimization_barrier((low_one, prepared))
    low_two = shifted(low_one, 1)
    up_two = shifted(up_one, -1)

    def grads(code, pair, chain, kind):
        return near_grads(code, pair, plan, prepared, comp_key, comp_value, chain, query.shape, kind)

    low_near, _ = lax.optimization_barrier((low_one, up_one))
    low_term, chain = grads(1, low_near, None, jnp.float32)
    low_two_term, chain = grads(0, low_two, chain, jnp.bfloat16)
    up_two_term, chain = grads(4, up_two, chain, jnp.bfloat16)
    low_two_term, up_two_term = lax.optimization_barrier((low_two_term, up_two_term))
    low_back = shifted(low_two_term, -1).astype(jnp.float32)
    up_back = shifted(up_two_term, 1).astype(jnp.float32)
    up_term, chain = grads(3, up_one, chain, jnp.float32)
    low_sum = (low_term + low_back).astype(jnp.bfloat16)
    up_sum = (up_term + up_back).astype(jnp.bfloat16)
    low_back = shifted(low_sum, -1).astype(jnp.float32)
    up_back = shifted(up_sum, 1).astype(jnp.float32)
    _, _, chain = lax.optimization_barrier((low_sum, up_sum, chain))
    own_term, chain = grads(2, own, chain, jnp.float32)
    gathered = (own_term + low_back + up_back).astype(jnp.bfloat16)
    back = lax.all_to_all(gathered, "mp", split_axis=0, concat_axis=0, tiled=True)
    key_back, value_back = join_heads(back)
    return chain[0], chain[1], chain[2], key_back[None], value_back[None]


def solution(mesh):
    return jax.shard_map(
        per_device,
        mesh=mesh,
        in_specs=(
            P("dp", None, "mp"),
            P("dp", None, "mp"),
            P("dp", None, "mp"),
            P("dp", "mp", None),
            P("dp", "mp", None),
            P("dp", None, "mp"),
            P(),
            P("dp"),
            P("dp"),
        ),
        out_specs=(
            P("dp", None, "mp"),
            P("dp", None, "mp"),
            P("dp", None, "mp"),
            P("dp", "mp", None),
            P("dp", "mp", None),
        ),
        check_vma=False,
    )
```
